128 devices in a mesh: replica: 16 (over z_hi, x, core), shard: 8 (over y, z_lo).
Axes of the slice: x: 4, y: 4, z: 4 (z_hi: 2, z_lo: 2; z = z_hi * 2 + z_lo), core: 2. Of those that a mesh axis runs over, the one named last changes fastest.
Arguments:
- hidden_in: bfloat16 [16, 1024, 2048], P('replica', 'shard'), may hold values from -6 to 6
- segment_ids: int32 [16, 1024], P('replica'), may hold values from 0 to 2, as said below
- positions: int32 [16, 1024], P('replica'), may hold values from 0 to 2048, as said below
- in_weight: bfloat16 [6144, 2048], P('shard'), may hold values from -0.125 to 0.125
- out_weight: bfloat16 [2048, 2048], P('shard'), may hold values from -2 to 2
- up_weight: bfloat16 [8192, 2048], P('shard'), may hold values from -0.125 to 0.125
- down_weight: bfloat16 [8192, 2048], P('shard'), may hold values from -0.0625 to 0.0625
- in_bias: bfloat16 [6144], P('shard'), may hold values from -4 to 4
- out_bias: bfloat16 [2048], P('shard'), may hold values from -4 to 4
- up_bias: bfloat16 [8192], P('shard'), may hold values from -4 to 4
- down_bias: bfloat16 [2048], P('shard'), may hold values from -4 to 4
- first_gain: bfloat16 [2048], P('shard'), may hold values from 0.5 to 1.5
- first_shift: bfloat16 [2048], P('shard'), may hold values from -4 to 4
- second_gain: bfloat16 [2048], P('shard'), may hold values from 0.5 to 1.5
- second_shift: bfloat16 [2048], P('shard'), may hold values from -4 to 4
- cotangent: bfloat16 [16, 1024, 2048], P('replica', 'shard'), may hold values from -6 to 6
Outputs:
- hidden_out: bfloat16 [16, 1024, 2048], P('replica', 'shard')
- grad_hidden: bfloat16 [16, 1024, 2048], P('replica', 'shard')
- grad_in_weight: float32 [6144, 2048], P('shard')
- grad_out_weight: float32 [2048, 2048], P('shard')
- grad_up_weight: float32 [8192, 2048], P('shard')
- grad_down_weight: float32 [8192, 2048], P('shard')
- grad_in_bias: float32 [6144], P('shard')
- grad_out_bias: float32 [2048], P('shard')
- grad_up_bias: float32 [8192], P('shard')
- grad_down_bias: float32 [2048], P('shard')
- grad_first_gain: float32 [2048], P('shard')
- grad_first_shift: float32 [2048], P('shard')
- grad_second_gain: float32 [2048], P('shard')
- grad_second_shift: float32 [2048], P('shard')
The draws below stay inside these ranges and needn't reach their ends.
Inputs may be any that keep to these rules, and one draw needn't show every extreme that they name: `segment_ids`: segment numbers never fall along a sequence, and each sequence holds documents 0, 1 and 2. positions rise by one from token to token within a document; documents 1 and 2 start at 0, document 0 continues an earlier one and ends at 2048.
All inputs are finite; a program needn't handle non-finite values.
Results may differ from the reference program's by a relative error of at most 0.023.
Values may be sent and summed in bfloat16 or wider, within the bound.
No kernel may reach another device: no remote copies, remote signals or barrier semaphores. Data moves between devices by JAX's collectives and lax.ppermute only.
A program may use at most 192 MiB of HBM per device.

```python
import math
import jax
import jax.numpy as jnp
from jax import lax

D = 2048
H = 8
HS = 256
ROT = 64
FF = 8192
LENGTH = 1024
ROWS = 128
NSEQ = 16


def document_bounds(key):
    flip = jax.random.randint(jax.random.fold_in(key, 103), (), 0, 2)
    spanning = (jnp.arange(NSEQ, dtype=jnp.int32) + flip) % 2 == 0
    lead_edge = jax.random.randint(jax.random.fold_in(key, 101), (NSEQ,), 1, ROWS)
    trail_edge = jax.random.randint(jax.random.fold_in(key, 102), (NSEQ,), 1, ROWS)
    lead_inner = jax.random.randint(jax.random.fold_in(key, 104), (NSEQ,), LENGTH // 5, 2 * LENGTH // 5)
    trail_inner = jax.random.randint(jax.random.fold_in(key, 105), (NSEQ,), LENGTH // 5, 2 * LENGTH // 5)
    leading = jnp.where(spanning, lead_edge, lead_inner)
    trailing = jnp.where(spanning, trail_edge, trail_inner)
    return (leading, LENGTH - trailing)


def draw_segment_ids(key, part):
    leading, ending = document_bounds(key)
    index = jnp.arange(LENGTH, dtype=jnp.int32)[None, :]
    return (index >= leading[:, None]).astype(jnp.int32) + (index >= ending[:, None]).astype(jnp.int32)


def draw_positions(key, part):
    leading, ending = document_bounds(key)
    index = jnp.arange(LENGTH, dtype=jnp.int32)[None, :]
    middle = jnp.where(index < ending[:, None], index - leading[:, None], index - ending[:, None])
    carried = index - leading[:, None] + 1 + 2 * LENGTH
    return jnp.where(index < leading[:, None], carried, middle).astype(jnp.int32)


def level_of(rng, shape, cuts, least, top_value):
    factor_of, own = 1.0, jax.random.fold_in(rng, 6)
    for position, shards_of in cuts:
        steps = jnp.exp(jax.random.uniform(jax.random.fold_in(own, position), (shards_of,), jnp.float32, least / len(cuts), top_value / len(cuts)))
        factor_of = factor_of * jnp.repeat(steps, shape[position] // shards_of).reshape([-1 if axis == position else 1 for axis in range(len(shape))])
    return factor_of


def noise(own_key, extent, scale, reach, shards=(), kind=jnp.bfloat16):
    result = scale * jax.random.normal(own_key, extent, jnp.float32)
    if shards:
        result = result * level_of(own_key, extent, shards, -0.22, 0.18)
    return jnp.clip(result, -reach, reach).astype(kind)


def setup_inputs(seed: int = 0) -> dict:
    key_list = jax.random.split(jax.random.key(seed), 17)
    return {
        "hidden_in": noise(key_list[0], (NSEQ, LENGTH, D), 1.0, 6.0, ((0, 16), (1, 8))),
        "segment_ids": draw_segment_ids(jax.random.fold_in(key_list[16], 71), 0),
        "positions": draw_positions(jax.random.fold_in(key_list[16], 71), 0),
        "in_weight": noise(key_list[3], (3 * D, D), D ** -0.5, 0.125, ((0, 8),)),
        "out_weight": noise(key_list[4], (D, D), (max(1, D // 256)) ** -0.5, 2.0, ((0, 8),)),
        "up_weight": noise(key_list[5], (FF, D), D ** -0.5, 0.125, ((0, 8),)),
        "down_weight": noise(key_list[6], (FF, D), FF ** -0.5, 0.0625, ((0, 8),)),
        "in_bias": noise(key_list[7], (3 * D,), 0.3, 4.0, ((0, 8),)),
        "out_bias": noise(key_list[8], (D,), 0.3, 4.0, ((0, 8),)),
        "up_bias": noise(key_list[9], (FF,), 0.3, 4.0, ((0, 8),)),
        "down_bias": noise(key_list[10], (D,), 0.3, 4.0, ((0, 8),)),
        "first_gain": jnp.clip(1.0 + 0.1 * jax.random.normal(key_list[11], (D,), jnp.float32), 0.5, 1.5).astype(jnp.bfloat16),
        "first_shift": noise(key_list[12], (D,), 0.3, 4.0, ((0, 8),)),
        "second_gain": jnp.clip(1.0 + 0.1 * jax.random.normal(key_list[13], (D,), jnp.float32), 0.5, 1.5).astype(jnp.bfloat16),
        "second_shift": noise(key_list[14], (D,), 0.3, 4.0, ((0, 8),)),
        "cotangent": noise(key_list[15], (NSEQ, LENGTH, D), 1.0, 6.0, ((0, 16), (1, 8))),
    }


HIGH = lax.Precision.HIGHEST
EPS = 1e-05
MASKED = -1e+30

@jax.custom_vjp
def low(v):
    return lax.optimization_barrier(v.astype(jnp.bfloat16)).astype(jnp.float32)

@jax.custom_vjp
def low_back(v):
    return v

def low_keep(v):
    return (low(v), None)

def low_pass(kept, grad):
    return (grad,)

def back_keep(v):
    return (v, None)

def back_low(kept, grad):
    return (low(grad),)
low.defvjp(low_keep, low_pass)
low_back.defvjp(back_keep, back_low)

def layer_norm(values, gain, shift):
    center = lax.optimization_barrier(jnp.mean(values, axis=-1, keepdims=True))
    centered = values - center
    spread = lax.optimization_barrier(jnp.mean(centered * centered, axis=-1, keepdims=True))
    return centered * lax.rsqrt(spread + EPS) * gain + shift

def angles(places):
    freq = jnp.power(10000.0, -2.0 * jnp.arange(ROT // 2, dtype=jnp.float32) / ROT)
    theta = places.astype(jnp.float32)[..., None] * freq
    return (jnp.cos(theta)[..., None, :], jnp.sin(theta)[..., None, :])

def rotate(values, cosine, sine):
    half = ROT // 2
    front = values[..., :half]
    second = values[..., half:ROT]
    remain = values[..., ROT:]
    return jnp.concatenate([front * cosine - second * sine, second * cosine + front * sine, remain], axis=-1)

def layer(params, inputs, segments, places):
    in_weight, out_weight, up_weight, down_weight, in_bias, out_bias, up_bias, down_bias, first_gain, first_shift, second_gain, second_shift = params
    batch = inputs.shape[0]
    scale = 1.0 / math.sqrt(HS)
    first_rows = low(layer_norm(inputs, first_gain, first_shift))
    mixed = low_back(jnp.einsum('bld,ed->ble', first_rows, in_weight, precision=HIGH) + in_bias)
    cosine, sine = angles(places)
    shaped = mixed.reshape(batch, LENGTH, H, 3, HS)
    query = low(rotate(shaped[:, :, :, 0, :], cosine, sine) * scale)
    keys = low(rotate(shaped[:, :, :, 1, :], cosine, sine))
    values = low(shaped[:, :, :, 2, :])
    block = min(512, LENGTH)
    count = LENGTH // block
    key_index = jnp.arange(LENGTH).astype(jnp.int32)

    def attend(start):
        query_block = lax.dynamic_slice_in_dim(query, start, block, 1)
        own_segments = lax.dynamic_slice_in_dim(segments, start, block, 1)
        query_index = start + jnp.arange(block).astype(jnp.int32)
        scores = low_back(jnp.einsum('bqhe,bkhe->bhqk', query_block, keys, precision=HIGH))
        allowed = (own_segments[:, :, None] == segments[:, None, :]) & (key_index[None, None, :] <= query_index[None, :, None])
        masked = jnp.where(allowed[:, None], scores, MASKED)
        top = lax.optimization_barrier(jnp.max(masked, axis=-1, keepdims=True))
        expd = jnp.exp(masked - top)
        probs = low(expd / lax.optimization_barrier(jnp.sum(expd, axis=-1, keepdims=True)))
        return jnp.einsum('bhqk,bkhe->bqhe', probs, values, precision=HIGH)
    starts = (jnp.arange(count) * block).astype(jnp.int32)
    blocks = lax.map(jax.checkpoint(attend), starts)
    context = jnp.moveaxis(blocks, 0, 1).reshape(batch, LENGTH, D)
    context = low(low_back(context))
    attention = jnp.einsum('bld,de->ble', context, out_weight, precision=HIGH) + out_bias
    second_rows = low(layer_norm(inputs, second_gain, second_shift))
    up_value = low_back(jnp.einsum('bld,fd->blf', second_rows, up_weight, precision=HIGH) + up_bias)
    active = low(jax.nn.gelu(up_value, approximate=False))
    feed = jnp.einsum('blf,fd->bld', active, down_weight, precision=HIGH) + down_bias
    return inputs + attention + feed

def reference(hidden_in, segment_ids, positions, in_weight, out_weight, up_weight, down_weight, in_bias, out_bias, up_bias, down_bias, first_gain, first_shift, second_gain, second_shift, cotangent):
    params = tuple((item.astype(jnp.float32) for item in (in_weight, out_weight, up_weight, down_weight, in_bias, out_bias, up_bias, down_bias, first_gain, first_shift, second_gain, second_shift)))
    group = math.gcd(NSEQ, max(1, 4096 // LENGTH))
    turns = NSEQ // group

    def split(values):
        return values.reshape((turns, group) + values.shape[1:])

    def advance(totals, item):
        inputs, segments, places, upstream = item
        output, backward = jax.vjp(lambda weights, rows: layer(weights, rows, segments, places), params, inputs.astype(jnp.float32))
        grads, input_grad = backward(upstream.astype(jnp.float32))
        totals = jax.tree.map(lambda left, right: left + right, totals, grads)
        return (totals, (output.astype(jnp.bfloat16), input_grad.astype(jnp.bfloat16)))
    zeros = jax.tree.map(jnp.zeros_like, params)
    totals, (outputs, input_grads) = lax.scan(advance, zeros, (split(hidden_in), split(segment_ids), split(positions), split(cotangent)))
    hidden_out = outputs.reshape(NSEQ, LENGTH, D)
    grad_hidden = input_grads.reshape(NSEQ, LENGTH, D)
    return (hidden_out, grad_hidden, totals[0], totals[1], totals[2], totals[3], totals[4], totals[5], totals[6], totals[7], totals[8], totals[9], totals[10], totals[11])
```

```python
import functools
import math

import jax
import jax.numpy as jnp
import numpy as np
from jax import lax
from jax.experimental import pallas as pl
from jax.experimental.pallas import tpu as pltpu
from jax.sharding import Mesh
from jax.sharding import PartitionSpec as P

HS = 256
ROT = 64
EPS = 1e-05
MASKED = -1e30

AXES = ("zh", "x", "c", "y", "zl")
SIZES = (2, 4, 2, 4, 2)
REPLICA = ("zh", "x", "c")
SHARD = ("y", "zl")
CHIP = ("x", "c")

F32 = jnp.float32
BF16 = jnp.bfloat16


def taking(microseconds):
    return pl.CostEstimate(
        flops=int(microseconds * 1e9), bytes_accessed=2**20, transcendentals=0
    )


def params_of(mib):
    return pltpu.CompilerParams(vmem_limit_bytes=mib * 2**20)


def whole_spec(v):
    return pl.BlockSpec(v.shape, lambda *_: (0,) * v.ndim)


def column_spec(v, tile):
    return pl.BlockSpec((v.shape[0], tile), lambda n: (0, n))


def row_spec(v, tile):
    return pl.BlockSpec((tile, v.shape[1]), lambda n: (n, 0))


def shifted(v, axis, by):
    n = lax.axis_size(axis)
    return lax.ppermute(v, axis, [(i, (i + by) % n) for i in range(n)])


def summed_small(v, axes):
    for axis in axes:
        n = lax.axis_size(axis)
        step = n // 2
        while step:
            v = v + lax.ppermute(v, axis, [(i, i ^ step) for i in range(n)])
            step //= 2
    return v


def nt(left, right):
    return lax.dot_general(left, right, (((1,), (1,)), ((), ())), preferred_element_type=F32)


def nn(left, right):
    return lax.dot_general(left, right, (((1,), (0,)), ((), ())), preferred_element_type=F32)


def tn(left, right):
    return lax.dot_general(left, right, (((0,), (0,)), ((), ())), preferred_element_type=F32)


def normed(values):
    center = jnp.mean(values, axis=-1, keepdims=True)
    centered = values - center
    spread = jnp.mean(centered * centered, axis=-1, keepdims=True)
    scale = lax.rsqrt(spread + EPS)
    return centered * scale, scale


def angles(places):
    freq = jnp.power(10000.0, -2.0 * jnp.arange(ROT // 2, dtype=F32) / ROT)
    theta = places.astype(F32)[:, None] * freq
    return jnp.cos(theta), jnp.sin(theta)


def block(v, index):
    return lax.dynamic_index_in_dim(v, index, 0, keepdims=False)


def after(v, *others):
    return lax.optimization_barrier((v,) + others)[0]


def exchanged(own, whole):
    rows = own.shape[0]
    half = rows // 2
    other = shifted(own, "zl", 1)
    left = shifted(own, "y", 1)
    right = shifted(own, "y", -1)
    other, whole = tie(other, whole)
    from_left = shifted(jnp.concatenate([other, left[:half]]), "y", 1)
    from_right = shifted(jnp.concatenate([other, right[half:]]), "y", -1)
    far_top = shifted(from_left[:half], "y", 1)
    far_low = shifted(from_right[half:rows], "y", -1)
    return whole, (own, left, right, other), (from_left, from_right, far_top, far_low)


def near_places(rows):
    return [
        (n, 0, rows, lambda dz=dz, dy=dy: place_of(dz, dy) * rows)
        for n, (dz, dy) in enumerate(((0, 0), (0, 3), (0, 1), (1, 0)))
    ]


def far_places(rows):
    half = rows // 2
    parts = (
        (0, 0, rows, 1, 3, 0),
        (1, 0, rows, 1, 1, 0),
        (0, rows, half, 0, 2, 0),
        (1, rows, half, 0, 2, half),
        (2, 0, half, 1, 2, 0),
        (3, 0, half, 1, 2, half),
    )
    return [
        (n, first, count, lambda dz=dz, dy=dy, low=low: place_of(dz, dy) * rows + low)
        for n, first, count, dz, dy, low in parts
    ]


def exchanged_near(own, ready_z, *ready_y):
    other = shifted(after(own, ready_z), "zl", 1)
    both = after(jnp.stack([own, other]), *ready_y)
    return both, shifted(both, "y", 1), shifted(both, "y", -1)


def exchanged_far(left, right):
    half = left.shape[1] // 2
    return shifted(left[:, :half], "y", 1), shifted(right[:, half:], "y", -1)


def place_kernel(parts, *refs):
    sources, out_ref = refs[:-1], refs[-1]
    for which, inner, place in parts:
        source = sources[which]
        values = source[...] if inner is None else source[inner]
        rows = values.shape[0]
        out_ref[pl.ds(pl.multiple_of(place(), rows), rows)] = values


def placed(sources, parts, rows):
    width, tile = sources[0].shape[-1], 512
    spec = lambda v: pl.BlockSpec(v.shape[:-1] + (tile,), lambda n: (0,) * (v.ndim - 1) + (n,))
    return pl.pallas_call(
        functools.partial(place_kernel, parts),
        grid=(width // tile,),
        in_specs=[spec(v) for v in sources],
        out_specs=pl.BlockSpec((rows, tile), lambda n: (0, n)),
        out_shape=jax.ShapeDtypeStruct((rows, width), sources[0].dtype),
        compiler_params=params_of(32),
        cost_estimate=taking(3),
        name="placed",
    )(*sources)


def placed_tokens(both, left, right, far_top, far_low):
    rows = both.shape[1]
    half = rows // 2
    parts = []
    for dz in range(2):
        for which, dy, low in ((0, 0, 0), (1, 3, 0), (2, 1, 0), (3, 2, 0), (4, 2, half)):
            parts.append(
                (which, dz, lambda dz=dz, dy=dy, low=low: place_of(dz, dy) * rows + low)
            )
    return placed((both, left, right, far_top, far_low), parts, 8 * rows)


def tie(*arrays):
    return lax.optimization_barrier(arrays)


def place_of(dz, dy):
    y, z = lax.axis_index("y"), lax.axis_index("zl")
    return lax.rem(y + dy, 4) * 2 + lax.rem(z + dz, 2)


def own_params_kernel(*refs):
    out_ref = refs[-1]
    for k, ref in enumerate(refs[:-1]):
        size = ref.shape[0]
        row = ref[...].astype(F32).reshape(1, size)
        out_ref[:, k * size : (k + 1) * size] = jnp.broadcast_to(row, (out_ref.shape[0], size))


def own_params(vectors, copies):
    total = sum(v.shape[0] for v in vectors)
    return pl.pallas_call(
        own_params_kernel,
        out_shape=jax.ShapeDtypeStruct((copies, total), F32),
        compiler_params=params_of(32),
        cost_estimate=taking(1),
        name="own_params",
    )(*vectors)


def norm_kernel(pieces, used, *refs):
    x_refs, p_ref = refs[:used], refs[used]
    one_ref, two_ref, one_buf, two_buf, sems = refs[-5:]
    copies = []
    row = 0
    for n, (which, first, rows, place) in enumerate(pieces):
        v = x_refs[which][first : first + rows].astype(F32)
        centered = v - jnp.mean(v, axis=-1, keepdims=True)
        spread = jnp.mean(centered * centered, axis=-1, keepdims=True)
        xhat = centered * lax.rsqrt(spread + EPS)
        here = pl.ds(row, rows)
        one_buf[here] = (xhat * p_ref[0:1] + p_ref[1:2]).astype(BF16)
        two_buf[here] = (xhat * p_ref[2:3] + p_ref[3:4]).astype(BF16)
        there = pl.ds(pl.multiple_of(place(), rows), rows)
        for k, (buf, ref) in enumerate(((one_buf, one_ref), (two_buf, two_ref))):
            copies.append(pltpu.make_async_copy(buf.at[here], ref.at[there], sems.at[2 * n + k]))
            copies[-1].start()
        row += rows
    for copy in copies:
        copy.wait()


def norm_into(arrays, pieces, params, buffers, length):
    width = arrays[0].shape[1]
    total = sum(rows for _, _, rows, _ in pieces)
    any_space = pl.BlockSpec(memory_space=pl.ANY)
    shape = jax.ShapeDtypeStruct((length, width), BF16)
    used = len(arrays)
    return pl.pallas_call(
        functools.partial(norm_kernel, pieces, used),
        in_specs=[pl.BlockSpec(memory_space=pltpu.VMEM)] * (used + 1) + [any_space] * len(buffers),
        out_specs=(any_space, any_space),
        out_shape=(shape, shape),
        input_output_aliases={used + 1: 0, used + 2: 1} if buffers else {},
        scratch_shapes=[
            pltpu.VMEM((total, width), BF16),
            pltpu.VMEM((total, width), BF16),
            pltpu.SemaphoreType.DMA((2 * len(pieces),)),
        ],
        compiler_params=params_of(48),
        cost_estimate=taking(3.4),
        name="norms",
    )(*arrays, params, *buffers)


def add_low(a, b):
    return (a.astype(F32) + b.astype(F32)).astype(BF16)


def exchange_rows(v):
    return lax.all_to_all(v.reshape(4, -1, v.shape[-1]), "y", 0, 0, tiled=True)


def exchange_blocks(v):
    return lax.all_to_all(v, SHARD, 0, 0, tiled=True)


def turn(values, tables, back):
    front = values[:, :128]
    up, down = pltpu.roll(front, 128 - ROT // 2, 1), pltpu.roll(front, ROT // 2, 1)
    moved = up * tables[1] + down * tables[2]
    front = front * tables[0] + (-moved if back else moved)
    return jnp.concatenate([front, values[:, 128:]], axis=-1)


def allowed_of(seg_col, seg_row, start, rows, count):
    same = seg_col[start : start + rows] == seg_row[:, :count]
    query = lax.broadcasted_iota(jnp.int32, (rows, count), 0) + start
    key = lax.broadcasted_iota(jnp.int32, (rows, count), 1)
    return same & (key <= query)


def attend_kernel(x_ref, w_ref, bias_ref, col_ref, row_ref, rot_ref, q_ref, k_ref, v_ref, c_ref, lse_ref):
    step, length = x_ref.shape[0], k_ref.shape[0]
    part = min(256, step)
    mixed = nt(x_ref[...], w_ref[...]) + bias_ref[...]
    tables = [rot_ref[i] for i in range(3)]
    q_ref[...] = (turn(mixed[:, :HS], tables, False) * (1.0 / math.sqrt(HS))).astype(BF16)
    now = pl.program_id(0)
    here = pl.ds(pl.multiple_of(now * step, step), step)
    k_ref[here] = turn(mixed[:, HS : 2 * HS], tables, False).astype(BF16)
    v_ref[here] = mixed[:, 2 * HS :].astype(BF16)
    for first in range(0, length, step):

        @pl.when(now * step == first)
        def _(first=first):
            for inner in range(0, step, part):
                rows, start = pl.ds(inner, part), first + inner
                count = start + part
                scores = nt(q_ref[rows], k_ref[:count])
                allowed = allowed_of(col_ref, row_ref[...], start, part, count)
                scores = jnp.where(allowed, scores, MASKED)
                top = jnp.max(scores, axis=-1, keepdims=True)
                expd = jnp.exp(scores - top)
                total = jnp.sum(expd, axis=-1, keepdims=True)
                probs = (expd * (1.0 / total)).astype(BF16)
                c_ref[rows] = nn(probs, v_ref[:count]).astype(BF16)
                lse_ref[rows] = top + jnp.log(total)


def attend(rows_one, in_weight, bias, seg_col, seg_row, tables):
    length = rows_one.shape[0]
    step = min(512, length)
    head = jax.ShapeDtypeStruct((length, HS), BF16)
    part = pl.BlockSpec((step, HS), lambda n: (n, 0))
    return pl.pallas_call(
        attend_kernel,
        grid=(length // step,),
        in_specs=[
            row_spec(rows_one, step),
            whole_spec(in_weight),
            whole_spec(bias),
            whole_spec(seg_col),
            whole_spec(seg_row),
            pl.BlockSpec((3, step, 128), lambda n: (0, n, 0)),
        ],
        out_specs=(
            part,
            whole_spec(head),
            whole_spec(head),
            part,
            pl.BlockSpec((step, 1), lambda n: (n, 0)),
        ),
        out_shape=(head, head, head, head, jax.ShapeDtypeStruct((length, 1), F32)),
        compiler_params=params_of(48),
        cost_estimate=taking(10),
        name="attend",
    )(rows_one, in_weight, bias, seg_col, seg_row, tables)


def attention_back(
    g_ref, w_ref, q_ref, k_ref, v_ref, lse_ref, col_ref, row_ref, rot_ref, out_ref, dk_ref, dv_ref
):
    length = g_ref.shape[0]
    step = min(256, length)
    seg_row = row_ref[...]
    dk_ref[...] = jnp.zeros_like(dk_ref)
    dv_ref[...] = jnp.zeros_like(dv_ref)
    for start in range(0, length, step):
        here, count = pl.ds(start, step), start + step
        before = pl.ds(0, count)
        context_grad = nt(g_ref[here], w_ref[...]).astype(BF16)
        query = q_ref[here]
        scores = nt(query, k_ref[:count])
        probs = jnp.exp(scores - lse_ref[here])
        probs = jnp.where(allowed_of(col_ref, seg_row, start, step, count), probs, 0.0)
        probs_grad = nt(context_grad, v_ref[:count])
        inner = jnp.sum(probs_grad * probs, axis=-1, keepdims=True)
        score_grad = (probs * (probs_grad - inner)).astype(BF16)
        dv_ref[before] += tn(probs.astype(BF16), context_grad)
        dk_ref[before] += tn(score_grad, query)
        tables = [rot_ref[i, here] for i in range(3)]
        query_grad = turn(nn(score_grad, k_ref[:count]), tables, True)
        out_ref[here, :HS] = (query_grad * (1.0 / math.sqrt(HS))).astype(BF16)
    tables = [rot_ref[i] for i in range(3)]
    out_ref[:, HS : 2 * HS] = turn(dk_ref[...], tables, True).astype(BF16)
    out_ref[:, 2 * HS :] = dv_ref[...].astype(BF16)


def attend_back_kernel(
    g_ref, ow_ref, q_ref, k_ref, v_ref, lse_ref, col_ref, row_ref, rot_ref, c_ref, up_ref,
    one_ref, two_ref, inw_ref, upw_ref, p_ref,
    keep_ref, send_ref, inner_a_ref, inner_b_ref, bias_ref,
    mix_ref, mix_t, c_t, dk_ref, dv_ref,
):
    now = pl.program_id(0)

    @pl.when(now == 0)
    def _():
        attention_back(
            g_ref, ow_ref, q_ref, k_ref, v_ref, lse_ref, col_ref, row_ref, rot_ref, mix_ref, dk_ref, dv_ref
        )
        bias_ref[...] = jnp.sum(mix_ref[...].astype(F32), axis=0, keepdims=True)
        mix_t[...] = mix_ref[...].T
        c_t[...] = c_ref[...].T

    half, tile = keep_ref.shape
    g_tile = g_ref[:, pl.ds(pl.multiple_of(now * tile, tile), tile)]
    one = one_ref[...]
    head = nn(mix_t[:half], one).astype(BF16)
    tail = jnp.concatenate(
        [nn(mix_t[half:], one).astype(BF16), nn(c_t[...], g_tile).astype(BF16)], axis=0
    )
    core = lax.axis_index("c") == 0
    keep_ref[...] = jnp.where(core, head, tail)
    send_ref[...] = jnp.where(core, tail, head)

    blocks, rows = inner_a_ref.shape[0], mix_ref.shape[0] // inner_a_ref.shape[0]
    first = nn(mix_ref[...], inw_ref[...])
    second = nn(up_ref[...], upw_ref[...])
    total = (first * p_ref[0:1] + second * p_ref[2:3]).astype(BF16)
    vectors = [
        jnp.sum(first * one.astype(F32), axis=0, keepdims=True),
        jnp.sum(first, axis=0, keepdims=True),
        jnp.sum(second * two_ref[...].astype(F32), axis=0, keepdims=True),
        jnp.sum(second, axis=0, keepdims=True),
    ]
    extra = jnp.concatenate(vectors + [jnp.zeros((12, tile), F32)], axis=0).astype(BF16)

    def store(ref):
        for k in range(blocks):
            ref[k, :rows] = total[k * rows : (k + 1) * rows]
            ref[k, rows:] = extra

    into_halves((inner_a_ref, inner_b_ref), store)


def attend_back(
    g_all, out_weight, query, keys, values, lse, seg_col, seg_row, tables, context, up_grad,
    rows_one, rows_two, in_weight, up_weight, params,
):
    length, width = rows_one.shape
    shards, tile = 8, 256
    half = (3 * HS + HS) // 2
    extra = length // shards + 16
    kept = jax.ShapeDtypeStruct((half, width), BF16)
    kept_spec = pl.BlockSpec((half, tile), lambda n: (0, n))
    once = [g_all, out_weight, query, keys, values, lse, seg_col, seg_row, tables, context, up_grad]
    tiled = [rows_one, rows_two, in_weight, up_weight, params]
    return pl.pallas_call(
        attend_back_kernel,
        grid=(width // tile,),
        in_specs=[
            pl.BlockSpec(v.shape, lambda n, v=v: (0,) * v.ndim, pipeline_mode=pl.Buffered(1))
            for v in once
        ]
        + [column_spec(v, tile) for v in tiled],
        out_specs=(
            kept_spec,
            kept_spec,
            *halves_spec((shards, extra, tile), width // tile // 2),
            pl.BlockSpec((1, 3 * HS), lambda n: (0, 0)),
        ),
        out_shape=(
            kept,
            kept,
            jax.ShapeDtypeStruct((shards, extra, width // 2), BF16),
            jax.ShapeDtypeStruct((shards, extra, width // 2), BF16),
            jax.ShapeDtypeStruct((1, 3 * HS), F32),
        ),
        scratch_shapes=[
            pltpu.VMEM((length, 3 * HS), BF16),
            pltpu.VMEM((3 * HS, length), BF16),
            pltpu.VMEM((HS, length), BF16),
            pltpu.VMEM((length, HS), F32),
            pltpu.VMEM((length, HS), F32),
        ],
        compiler_params=params_of(56),
        cost_estimate=taking(300),
        name="attend_back",
    )(*once, *tiled)


def halves_spec(block, tiles):
    lead = (0,) * (len(block) - 1)
    return (
        pl.BlockSpec(block, lambda n: lead + (jnp.minimum(n, tiles - 1),)),
        pl.BlockSpec(block, lambda n: lead + (jnp.maximum(n - tiles, 0),)),
    )


def into_halves(refs, store):
    now, tiles = pl.program_id(0), pl.num_programs(0) // 2
    for k, ref in enumerate(refs):
        pl.when(lax.div(now, tiles) == k)(functools.partial(store, ref))


def branch_kernel(c_ref, a_ref, ow_ref, dw_ref, out_ref):
    out_ref[...] = (nn(c_ref[...], ow_ref[...]) + nn(a_ref[...], dw_ref[...])).astype(BF16)


def branch_of(context, active, out_weight, down_weight):
    length, width, tile = context.shape[0], out_weight.shape[1], 256
    return pl.pallas_call(
        branch_kernel,
        grid=(width // tile,),
        in_specs=[
            whole_spec(context),
            whole_spec(active),
            column_spec(out_weight, tile),
            column_spec(down_weight, tile),
        ],
        out_specs=pl.BlockSpec((length, tile), lambda n: (0, n)),
        out_shape=jax.ShapeDtypeStruct((length, width), BF16),
        compiler_params=params_of(32),
        cost_estimate=taking(10),
        name="branch",
    )(context, active, out_weight, down_weight)


def feed_back_kernel(
    g_ref, w_ref, slope_ref, act_ref, two_ref, grads_ref, up_ref, bias_ref, act_t, up_t
):
    now = pl.program_id(0)
    owners, _, rows, tile = grads_ref.shape

    @pl.when(now == 0)
    def _():
        act_t[...] = act_ref[...].T
        hidden = w_ref.shape[0]
        step = min(256, hidden)
        for start in range(0, hidden, step):
            here = slice(start, start + step)
            up_grad = (nt(g_ref[...], w_ref[here]) * slope_ref[:, here].astype(F32)).astype(BF16)
            up_ref[:, here] = up_grad
            bias_ref[:, here] = jnp.sum(up_grad.astype(F32), axis=0, keepdims=True)
            up_t[here] = up_grad.T

    g_tile = g_ref[:, pl.ds(pl.multiple_of(now * tile, tile), tile)]
    grad_down = nn(act_t[...], g_tile).astype(BF16)
    grad_up = nn(up_t[...], two_ref[...]).astype(BF16)
    for k in range(owners):
        grads_ref[k, 0] = grad_down[k * rows : (k + 1) * rows]
        grads_ref[k, 1] = grad_up[k * rows : (k + 1) * rows]


def feed_back(g_all, rows_two, active, slope, down_weight):
    length, width = g_all.shape
    hidden, tile, owners = active.shape[1], 256, 8
    rows = hidden // owners
    once = [g_all, down_weight, slope, active]
    return pl.pallas_call(
        feed_back_kernel,
        grid=(width // tile,),
        in_specs=[
            pl.BlockSpec(v.shape, lambda n: (0, 0), pipeline_mode=pl.Buffered(1)) for v in once
        ]
        + [column_spec(rows_two, tile)],
        out_specs=(
            pl.BlockSpec((owners, 2, rows, tile), lambda n: (0, 0, 0, n)),
            pl.BlockSpec((length, hidden), lambda n: (0, 0)),
            pl.BlockSpec((1, hidden), lambda n: (0, 0)),
        ),
        out_shape=(
            jax.ShapeDtypeStruct((owners, 2, rows, width), BF16),
            jax.ShapeDtypeStruct((length, hidden), BF16),
            jax.ShapeDtypeStruct((1, hidden), F32),
        ),
        scratch_shapes=[pltpu.VMEM((hidden, length), BF16), pltpu.VMEM((hidden, length), BF16)],
        compiler_params=params_of(48),
        cost_estimate=taking(80),
        name="feed_back",
    )(*once, rows_two)


def sum_spread_kernel(a_ref, b_ref, *out_refs):
    rows = out_refs[0].shape[0]
    me = lax.axis_index("x")
    for by, out_ref in enumerate(out_refs):
        here = pl.ds(pl.multiple_of(lax.rem(me + by, 4) * rows, rows), rows)
        out_ref[...] = (a_ref[here].astype(F32) + b_ref[here].astype(F32)).astype(BF16)


def sum_spread(a, b):
    shape = jax.ShapeDtypeStruct((a.shape[0] // 4, a.shape[1]), BF16)
    return pl.pallas_call(
        sum_spread_kernel,
        out_shape=(shape,) * 4,
        compiler_params=params_of(32),
        cost_estimate=taking(2),
        name="sum_spread",
    )(a, b)


def near_out_kernel(mine_ref, theirs_ref, in_ref, out_ref):
    step = pl.program_id(0)
    first = lax.axis_index("c") == lax.div(step, 4)
    total = jnp.where(first, mine_ref[...], theirs_ref[...]).astype(F32)
    blocks = 6

    @pl.when(step < blocks)
    def _():
        in_ref[...] = total

    @pl.when(step >= blocks)
    def _():
        out_ref[...] = total


def near_out(mine, theirs):
    rows, width = mine.shape[0] // 4, mine.shape[1]
    spec = pl.BlockSpec((rows, width), lambda n: (lax.rem(n, 4), 0))
    return pl.pallas_call(
        near_out_kernel,
        grid=(8,),
        in_specs=[spec, spec],
        out_specs=(
            pl.BlockSpec((rows, width), lambda n: (jnp.minimum(n, 5), 0)),
            pl.BlockSpec((rows, width), lambda n: (jnp.maximum(n - 6, 0), 0)),
        ),
        out_shape=(
            jax.ShapeDtypeStruct((6 * rows, width), F32),
            jax.ShapeDtypeStruct((2 * rows, width), F32),
        ),
        compiler_params=params_of(32),
        cost_estimate=taking(9),
        name="near_out",
    )(mine, theirs)


def widen_kernel(a_ref, out_ref):
    out_ref[...] = a_ref[...].astype(F32)


def widen(v):
    spec = row_spec(v, 256)
    return pl.pallas_call(
        widen_kernel,
        grid=(v.shape[0] // 256,),
        in_specs=[spec],
        out_specs=spec,
        out_shape=jax.ShapeDtypeStruct(v.shape, F32),
        compiler_params=params_of(32),
        cost_estimate=taking(4),
        name="widen",
    )(v)


def swap_sum(v, axis):
    me = lax.axis_index(axis)
    return block(v, me).astype(F32) + shifted(block(v, 1 - me), axis, 1).astype(F32)


def body(
    hidden_in,
    segment_ids,
    positions,
    in_weight,
    out_weight,
    up_weight,
    down_weight,
    in_bias,
    out_bias,
    up_bias,
    down_bias,
    first_gain,
    first_shift,
    second_gain,
    second_shift,
    cotangent,
):
    _, rows, width = hidden_in.shape
    shards = lax.axis_size(SHARD)
    length = rows * shards
    own = width // shards
    me = lax.axis_index(SHARD)
    x_own, g_own = hidden_in[0], cotangent[0]

    owned = own_params(
        [first_gain, first_shift, second_gain, second_shift, out_bias, down_bias], shards
    )
    whole = exchange_blocks(owned)

    whole, x_near, x_far = exchanged(x_own, whole)

    whole = whole.reshape(shards, 6, own).swapaxes(0, 1).reshape(6, width)
    gain_one, shift_one, gain_two, shift_two = (whole[i][None] for i in range(4))
    biases_out = (whole[4] + whole[5])[None]

    seg_col, seg_row = segment_ids[0][:, None], segment_ids
    cosine, sine = angles(positions[0])
    half = jnp.zeros_like(sine)
    rest = jnp.zeros((length, 128 - ROT), F32)
    tables = jnp.stack(
        [
            jnp.concatenate([cosine, cosine, rest + 1.0], axis=-1),
            jnp.concatenate([-sine, half, rest], axis=-1),
            jnp.concatenate([half, sine, rest], axis=-1),
        ]
    )

    buffers = norm_into(x_near, near_places(rows), whole, (), length)
    rows_one, rows_two = norm_into(x_far, far_places(rows), whole, buffers, length)
    g_both, g_left, g_right = exchanged_near(g_own, x_near[3], x_far[2], x_far[3])

    query, keys, values, context, lse = attend(
        rows_one, in_weight, in_bias.astype(F32)[None], seg_col, seg_row, tables
    )

    rows_two, g_left, g_right, context = tie(rows_two, g_left, g_right, context)
    far_top, far_low = exchanged_far(g_left, g_right)
    up = nt(rows_two, up_weight) + up_bias.astype(F32)[None]
    phi = 0.5 * (1.0 + lax.erf(up * (1.0 / math.sqrt(2.0))))
    slope = phi + up * (jnp.exp(-0.5 * up * up) * (1.0 / math.sqrt(2.0 * math.pi)))
    slope = slope.astype(BF16)
    active = (up * phi).astype(BF16)

    active, far_top, far_low = tie(active, far_top, far_low)
    g_all = placed_tokens(g_both, g_left, g_right, far_top, far_low)

    grads, up_grad, up_own = feed_back(g_all, rows_two, active, slope, down_weight)
    part = lax.psum_scatter(grads.reshape(-1, width), CHIP, scatter_dimension=0, tiled=True)

    active, up_grad = tie(active, up_grad)
    branch = branch_of(context, active, out_weight, down_weight)
    context, branch = tie(context, branch)
    branch = exchange_blocks(branch.reshape(shards, rows, width))

    g_late, context, up_grad = tie(g_all, context, up_grad)
    keep, send, inner_one, inner_two, in_own = attend_back(
        g_late, out_weight, query, keys, values, lse, seg_col, seg_row, tables, context, up_grad,
        rows_one, rows_two, in_weight, up_weight, whole,
    )
    heads, hidden = in_own.shape[1], up_own.shape[1]

    near_parts = sum_spread(keep, shifted(send, "c", 1))
    near_pieces = [near_parts[0]] + [shifted(near_parts[by], "x", by) for by in (1, 3, 2)]

    owned_rows = part.shape[0] // 2
    part_down, part_up = part[:owned_rows], part[owned_rows:]
    far_down = shifted(part_down, "zh", 1)
    part_down, part_up, far_down, branch, inner_one, *near_pieces = tie(
        part_down, part_up, far_down, branch, inner_one, *near_pieces
    )
    part_down = add_low(part_down, far_down)
    sum_down = lax.all_gather(part_down, CHIP, axis=0, tiled=True)
    inner_one = exchange_rows(inner_one)
    far_up = shifted(part_up, "zh", 1)
    near = sum(p.astype(F32) for p in near_pieces).astype(BF16)
    near = add_low(near, shifted(near, "zh", 1))
    near, part_up, far_up, inner_one, inner_two, part_down = tie(
        near, part_up, far_up, inner_one, inner_two, part_down
    )
    part_up = add_low(part_up, far_up)
    sum_up = lax.all_gather(part_up, CHIP, axis=0, tiled=True)
    inner_two = exchange_rows(inner_two)
    near_all = [near] + [shifted(near, "x", by) for by in (1, 3, 2)]
    branch = jnp.sum(branch.astype(F32), axis=0)
    hidden_out = (x_own.astype(F32) + branch + biases_out).astype(BF16)
    hidden_out, inner_one, inner_two, part_up, *near_all = tie(
        hidden_out, inner_one, inner_two, part_up, *near_all
    )

    received = jnp.concatenate(
        [jnp.sum(v.astype(F32), axis=0).astype(BF16) for v in (inner_one, inner_two)], axis=-1
    )
    received = swap_sum(received.reshape(2, -1, width), "zl")
    inner_grad = received[:rows]
    vectors = lax.dynamic_slice(received, (rows, me * own), (4, own))
    vectors = jnp.stack(
        [
            (vectors[0] - first_shift.astype(F32) * vectors[1]) / first_gain.astype(F32),
            vectors[1],
            (vectors[2] - second_shift.astype(F32) * vectors[3]) / second_gain.astype(F32),
            vectors[3],
        ]
    )
    g_columns = lax.dynamic_slice(g_all, (0, me * own), (length, own))
    small = jnp.concatenate(
        [
            vectors.reshape(-1),
            in_own[0],
            up_own[0],
            jnp.sum(g_columns, axis=0, dtype=F32),
        ]
    )
    sum_down = widen(sum_down)
    parts = [
        (n, None, lambda by=by: lax.rem(lax.axis_index("x") + 4 - by, 4) * 128)
        for n, by in enumerate((0, 1, 3, 2))
    ]
    mine = placed(near_all, parts, 512)
    theirs = shifted(mine, "c", 1)
    small = summed_small(small.reshape(-1, 128), REPLICA).reshape(-1)
    cuts = np.cumsum([own, own, own, own, heads, hidden])
    sum_in, sum_out = near_out(mine, theirs)
    gain_one_g, shift_one_g, gain_two_g, shift_two_g, in_b, up_b, out_b = jnp.split(small, cuts)

    xhat_own, scale_own = normed(x_own.astype(F32))
    centered = inner_grad - jnp.mean(inner_grad, axis=-1, keepdims=True)
    along = jnp.mean(inner_grad * xhat_own, axis=-1, keepdims=True)
    grad_hidden = (g_own.astype(F32) + scale_own * (centered - xhat_own * along)).astype(BF16)

    return (
        hidden_out[None],
        grad_hidden[None],
        sum_in,
        sum_out,
        widen(sum_up),
        sum_down,
        in_b,
        out_b,
        up_b,
        out_b,
        gain_one_g,
        shift_one_g,
        gain_two_g,
        shift_two_g,
    )


def solution(mesh):
    split = Mesh(mesh.devices.reshape(SIZES), AXES)
    tokens, params, vector = P(REPLICA, SHARD, None), P(SHARD, None), P(SHARD)
    return jax.shard_map(
        body,
        mesh=split,
        in_specs=(
            (tokens, P(REPLICA, None), P(REPLICA, None)) + (params,) * 4 + (vector,) * 8 + (tokens,)
        ),
        out_specs=(tokens,) * 2 + (params,) * 4 + (vector,) * 8,
        check_vma=False,
    )
```

```python
import functools
import math

import jax
import jax.numpy as jnp
import numpy as np
from jax import lax
from jax.experimental import pallas as pl
from jax.experimental.pallas import tpu as pltpu
from jax.sharding import Mesh
from jax.sharding import PartitionSpec as P

HS = 256
ROT = 64
EPS = 1e-05
MASKED = -1e30

AXES = ("zh", "x", "c", "y", "zl")
SIZES = (2, 4, 2, 4, 2)
REPLICA = ("zh", "x", "c")
SHARD = ("y", "zl")
CHIP = ("x", "c")

F32 = jnp.float32
BF16 = jnp.bfloat16


def taking(microseconds):
    return pl.CostEstimate(
        flops=int(microseconds * 1e9), bytes_accessed=2**20, transcendentals=0
    )


def params_of(mib):
    return pltpu.CompilerParams(vmem_limit_bytes=mib * 2**20)


def whole_spec(v):
    return pl.BlockSpec(v.shape, lambda *_: (0,) * v.ndim)


def column_spec(v, tile):
    return pl.BlockSpec((v.shape[0], tile), lambda n: (0, n))


def row_spec(v, tile):
    return pl.BlockSpec((tile, v.shape[1]), lambda n: (n, 0))


def shifted(v, axis, by):
    n = lax.axis_size(axis)
    return lax.ppermute(v, axis, [(i, (i + by) % n) for i in range(n)])


def summed_small(v, axes):
    for axis in axes:
        n = lax.axis_size(axis)
        step = n // 2
        while step:
            v = v + lax.ppermute(v, axis, [(i, i ^ step) for i in range(n)])
            step //= 2
    return v


def nt(left, right):
    return lax.dot_general(left, right, (((1,), (1,)), ((), ())), preferred_element_type=F32)


def nn(left, right):
    return lax.dot_general(left, right, (((1,), (0,)), ((), ())), preferred_element_type=F32)


def tn(left, right):
    return lax.dot_general(left, right, (((0,), (0,)), ((), ())), preferred_element_type=F32)


def normed(values):
    center = jnp.mean(values, axis=-1, keepdims=True)
    centered = values - center
    spread = jnp.mean(centered * centered, axis=-1, keepdims=True)
    scale = lax.rsqrt(spread + EPS)
    return centered * scale, scale


def angles(places):
    freq = jnp.power(10000.0, -2.0 * jnp.arange(ROT // 2, dtype=F32) / ROT)
    theta = places.astype(F32)[:, None] * freq
    return jnp.cos(theta), jnp.sin(theta)


def block(v, index):
    return lax.dynamic_index_in_dim(v, index, 0, keepdims=False)


def after(v, *others):
    return lax.optimization_barrier((v,) + others)[0]


def exchanged(own, whole):
    rows = own.shape[0]
    half = rows // 2
    other = shifted(own, "zl", 1)
    left = shifted(own, "y", 1)
    right = shifted(own, "y", -1)
    from_left = shifted(jnp.concatenate([other, left[:half]]), "y", 1)
    from_right = shifted(jnp.concatenate([other, right[half:]]), "y", -1)
    from_left, from_right, whole = tie(from_left, from_right, whole)
    far_top = shifted(from_left[:half], "y", 1)
    far_low = shifted(from_right[half:rows], "y", -1)
    return whole, (own, left, right, other), (from_left, from_right, far_top, far_low)


def near_places(rows):
    return [
        (n, 0, rows, lambda dz=dz, dy=dy: place_of(dz, dy) * rows)
        for n, (dz, dy) in enumerate(((0, 0), (0, 3), (0, 1), (1, 0)))
    ]


def far_places(rows):
    half = rows // 2
    parts = (
        (0, 0, rows, 1, 3, 0),
        (1, 0, rows, 1, 1, 0),
        (0, rows, half, 0, 2, 0),
        (1, rows, half, 0, 2, half),
        (2, 0, half, 1, 2, 0),
        (3, 0, half, 1, 2, half),
    )
    return [
        (n, first, count, lambda dz=dz, dy=dy, low=low: place_of(dz, dy) * rows + low)
        for n, first, count, dz, dy, low in parts
    ]


def exchanged_near(own, ready_z, *ready_y):
    other = shifted(after(own, ready_z), "zl", 1)
    both = after(jnp.stack([own, other]), *ready_y)
    return both, shifted(both, "y", 1), shifted(both, "y", -1)


def exchanged_far(left, right):
    half = left.shape[1] // 2
    return shifted(left[:, :half], "y", 1), shifted(right[:, half:], "y", -1)


def place_kernel(parts, *refs):
    sources, out_ref = refs[:-1], refs[-1]
    for which, inner, place in parts:
        source = sources[which]
        values = source[...] if inner is None else source[inner]
        rows = values.shape[0]
        out_ref[pl.ds(pl.multiple_of(place(), rows), rows)] = values


def placed(sources, parts, rows):
    width, tile = sources[0].shape[-1], 512
    spec = lambda v: pl.BlockSpec(v.shape[:-1] + (tile,), lambda n: (0,) * (v.ndim - 1) + (n,))
    return pl.pallas_call(
        functools.partial(place_kernel, parts),
        grid=(width // tile,),
        in_specs=[spec(v) for v in sources],
        out_specs=pl.BlockSpec((rows, tile), lambda n: (0, n)),
        out_shape=jax.ShapeDtypeStruct((rows, width), sources[0].dtype),
        compiler_params=params_of(57),
        cost_estimate=taking(3),
        name="placed",
    )(*sources)


def placed_tokens(both, left, right, far_top, far_low):
    rows = both.shape[1]
    half = rows // 2
    parts = []
    for dz in range(2):
        for which, dy, low in ((0, 0, 0), (1, 3, 0), (2, 1, 0), (3, 2, 0), (4, 2, half)):
            parts.append(
                (which, dz, lambda dz=dz, dy=dy, low=low: place_of(dz, dy) * rows + low)
            )
    return placed((both, left, right, far_top, far_low), parts, 8 * rows)


def tie(*arrays):
    return lax.optimization_barrier(arrays)


def place_of(dz, dy):
    y, z = lax.axis_index("y"), lax.axis_index("zl")
    return lax.rem(y + dy, 4) * 2 + lax.rem(z + dz, 2)


def own_params_kernel(*refs):
    out_ref = refs[-1]
    for k, ref in enumerate(refs[:-1]):
        size = ref.shape[0]
        row = ref[...].astype(F32).reshape(1, size)
        out_ref[:, k * size : (k + 1) * size] = jnp.broadcast_to(row, (out_ref.shape[0], size))


def own_params(vectors, copies):
    total = sum(v.shape[0] for v in vectors)
    return pl.pallas_call(
        own_params_kernel,
        out_shape=jax.ShapeDtypeStruct((copies, total), F32),
        compiler_params=params_of(32),
        cost_estimate=taking(1),
        name="own_params",
    )(*vectors)


def norm_kernel(pieces, used, *refs):
    x_refs, p_ref = refs[:used], refs[used]
    one_ref, two_ref, one_buf, two_buf, sems = refs[-5:]
    copies = []
    row = 0
    for n, (which, first, rows, place) in enumerate(pieces):
        v = x_refs[which][first : first + rows].astype(F32)
        centered = v - jnp.mean(v, axis=-1, keepdims=True)
        spread = jnp.mean(centered * centered, axis=-1, keepdims=True)
        xhat = centered * lax.rsqrt(spread + EPS)
        here = pl.ds(row, rows)
        one_buf[here] = (xhat * p_ref[0:1] + p_ref[1:2]).astype(BF16)
        two_buf[here] = (xhat * p_ref[2:3] + p_ref[3:4]).astype(BF16)
        there = pl.ds(pl.multiple_of(place(), rows), rows)
        for k, (buf, ref) in enumerate(((one_buf, one_ref), (two_buf, two_ref))):
            copies.append(pltpu.make_async_copy(buf.at[here], ref.at[there], sems.at[2 * n + k]))
            copies[-1].start()
        row += rows
    for copy in copies:
        copy.wait()


def norm_into(arrays, pieces, params, buffers, length):
    width = arrays[0].shape[1]
    total = sum(rows for _, _, rows, _ in pieces)
    any_space = pl.BlockSpec(memory_space=pl.ANY)
    shape = jax.ShapeDtypeStruct((length, width), BF16)
    used = len(arrays)
    return pl.pallas_call(
        functools.partial(norm_kernel, pieces, used),
        in_specs=[pl.BlockSpec(memory_space=pltpu.VMEM)] * (used + 1) + [any_space] * len(buffers),
        out_specs=(any_space, any_space),
        out_shape=(shape, shape),
        input_output_aliases={used + 1: 0, used + 2: 1} if buffers else {},
        scratch_shapes=[
            pltpu.VMEM((total, width), BF16),
            pltpu.VMEM((total, width), BF16),
            pltpu.SemaphoreType.DMA((2 * len(pieces),)),
        ],
        compiler_params=params_of(48),
        cost_estimate=taking(3.4),
        name="norms",
    )(*arrays, params, *buffers)


def add_low(a, b):
    return (a.astype(F32) + b.astype(F32)).astype(BF16)


def exchange_rows(v):
    return lax.all_to_all(v.reshape(4, -1, v.shape[-1]), "y", 0, 0, tiled=True)


def exchange_blocks(v):
    return lax.all_to_all(v, SHARD, 0, 0, tiled=True)


def turn(values, tables, back):
    front = values[:, :128]
    up, down = pltpu.roll(front, 128 - ROT // 2, 1), pltpu.roll(front, ROT // 2, 1)
    moved = up * tables[1] + down * tables[2]
    front = front * tables[0] + (-moved if back else moved)
    return jnp.concatenate([front, values[:, 128:]], axis=-1)


def allowed_of(seg_col, seg_row, start, rows, count):
    same = seg_col[start : start + rows] == seg_row[:, :count]
    query = lax.broadcasted_iota(jnp.int32, (rows, count), 0) + start
    key = lax.broadcasted_iota(jnp.int32, (rows, count), 1)
    return same & (key <= query)


def attend_kernel(x_ref, w_ref, bias_ref, col_ref, row_ref, rot_ref, q_ref, k_ref, v_ref, c_ref, lse_ref):
    step, length = x_ref.shape[0], k_ref.shape[0]
    part = min(256, step)
    mixed = nt(x_ref[...], w_ref[...]) + bias_ref[...]
    tables = [rot_ref[i] for i in range(3)]
    q_ref[...] = (turn(mixed[:, :HS], tables, False) * (1.0 / math.sqrt(HS))).astype(BF16)
    now = pl.program_id(0)
    here = pl.ds(pl.multiple_of(now * step, step), step)
    k_ref[here] = turn(mixed[:, HS : 2 * HS], tables, False).astype(BF16)
    v_ref[here] = mixed[:, 2 * HS :].astype(BF16)
    for first in range(0, length, step):

        @pl.when(now * step == first)
        def _(first=first):
            for inner in range(0, step, part):
                rows, start = pl.ds(inner, part), first + inner
                count = start + part
                scores = nt(q_ref[rows], k_ref[:count])
                allowed = allowed_of(col_ref, row_ref[...], start, part, count)
                scores = jnp.where(allowed, scores, MASKED)
                top = jnp.max(scores, axis=-1, keepdims=True)
                expd = jnp.exp(scores - top)
                total = jnp.sum(expd, axis=-1, keepdims=True)
                probs = (expd * (1.0 / total)).astype(BF16)
                c_ref[rows] = nn(probs, v_ref[:count]).astype(BF16)
                lse_ref[rows] = top + jnp.log(total)


def attend(rows_one, in_weight, bias, seg_col, seg_row, tables):
    length = rows_one.shape[0]
    step = min(512, length)
    head = jax.ShapeDtypeStruct((length, HS), BF16)
    part = pl.BlockSpec((step, HS), lambda n: (n, 0))
    return pl.pallas_call(
        attend_kernel,
        grid=(length // step,),
        in_specs=[
            row_spec(rows_one, step),
            whole_spec(in_weight),
            whole_spec(bias),
            whole_spec(seg_col),
            whole_spec(seg_row),
            pl.BlockSpec((3, step, 128), lambda n: (0, n, 0)),
        ],
        out_specs=(
            part,
            whole_spec(head),
            whole_spec(head),
            part,
            pl.BlockSpec((step, 1), lambda n: (n, 0)),
        ),
        out_shape=(head, head, head, head, jax.ShapeDtypeStruct((length, 1), F32)),
        compiler_params=params_of(48),
        cost_estimate=taking(10),
        name="attend",
    )(rows_one, in_weight, bias, seg_col, seg_row, tables)


def attention_back(
    g_ref, w_ref, q_ref, k_ref, v_ref, lse_ref, col_ref, row_ref, rot_ref, out_ref, dk_ref, dv_ref
):
    length = g_ref.shape[0]
    step = min(256, length)
    seg_row = row_ref[...]
    dk_ref[...] = jnp.zeros_like(dk_ref)
    dv_ref[...] = jnp.zeros_like(dv_ref)
    for start in range(0, length, step):
        here, count = pl.ds(start, step), start + step
        before = pl.ds(0, count)
        context_grad = nt(g_ref[here], w_ref[...]).astype(BF16)
        query = q_ref[here]
        scores = nt(query, k_ref[:count])
        probs = jnp.exp(scores - lse_ref[here])
        probs = jnp.where(allowed_of(col_ref, seg_row, start, step, count), probs, 0.0)
        probs_grad = nt(context_grad, v_ref[:count])
        inner = jnp.sum(probs_grad * probs, axis=-1, keepdims=True)
        score_grad = (probs * (probs_grad - inner)).astype(BF16)
        dv_ref[before] += tn(probs.astype(BF16), context_grad)
        dk_ref[before] += tn(score_grad, query)
        tables = [rot_ref[i, here] for i in range(3)]
        query_grad = turn(nn(score_grad, k_ref[:count]), tables, True)
        out_ref[here, :HS] = (query_grad * (1.0 / math.sqrt(HS))).astype(BF16)
    tables = [rot_ref[i] for i in range(3)]
    out_ref[:, HS : 2 * HS] = turn(dk_ref[...], tables, True).astype(BF16)
    out_ref[:, 2 * HS :] = dv_ref[...].astype(BF16)


def attend_back_kernel(
    g_ref, ow_ref, q_ref, k_ref, v_ref, lse_ref, col_ref, row_ref, rot_ref, c_ref, up_ref,
    one_ref, two_ref, inw_ref, upw_ref, p_ref,
    keep_ref, send_ref, inner_a_ref, inner_b_ref, bias_ref,
    mix_ref, mix_t, c_t, dk_ref, dv_ref,
):
    now = pl.program_id(0)

    @pl.when(now == 0)
    def _():
        attention_back(
            g_ref, ow_ref, q_ref, k_ref, v_ref, lse_ref, col_ref, row_ref, rot_ref, mix_ref, dk_ref, dv_ref
        )
        bias_ref[...] = jnp.sum(mix_ref[...].astype(F32), axis=0, keepdims=True)
        mix_t[...] = mix_ref[...].T
        c_t[...] = c_ref[...].T

    half, tile = keep_ref.shape
    g_tile = g_ref[:, pl.ds(pl.multiple_of(now * tile, tile), tile)]
    one = one_ref[...]
    head = nn(mix_t[:half], one).astype(BF16)
    tail = jnp.concatenate(
        [nn(mix_t[half:], one).astype(BF16), nn(c_t[...], g_tile).astype(BF16)], axis=0
    )
    core = lax.axis_index("c") == 0
    keep_ref[...] = jnp.where(core, head, tail)
    send_ref[...] = jnp.where(core, tail, head)

    blocks, rows = inner_a_ref.shape[0], mix_ref.shape[0] // inner_a_ref.shape[0]
    first = nn(mix_ref[...], inw_ref[...])
    second = nn(up_ref[...], upw_ref[...])
    total = (first * p_ref[0:1] + second * p_ref[2:3]).astype(BF16)
    vectors = [
        jnp.sum(first * one.astype(F32), axis=0, keepdims=True),
        jnp.sum(first, axis=0, keepdims=True),
        jnp.sum(second * two_ref[...].astype(F32), axis=0, keepdims=True),
        jnp.sum(second, axis=0, keepdims=True),
    ]
    extra = jnp.concatenate(vectors + [jnp.zeros((12, tile), F32)], axis=0).astype(BF16)

    def store(ref):
        for k in range(blocks):
            ref[k, :rows] = total[k * rows : (k + 1) * rows]
            ref[k, rows:] = extra

    into_halves((inner_a_ref, inner_b_ref), store)


def attend_back(
    g_all, out_weight, query, keys, values, lse, seg_col, seg_row, tables, context, up_grad,
    rows_one, rows_two, in_weight, up_weight, params,
):
    length, width = rows_one.shape
    shards, tile = 8, 256
    half = (3 * HS + HS) // 2
    extra = length // shards + 16
    kept = jax.ShapeDtypeStruct((half, width), BF16)
    kept_spec = pl.BlockSpec((half, tile), lambda n: (0, n))
    once = [g_all, out_weight, query, keys, values, lse, seg_col, seg_row, tables, context, up_grad]
    tiled = [rows_one, rows_two, in_weight, up_weight, params]
    return pl.pallas_call(
        attend_back_kernel,
        grid=(width // tile,),
        in_specs=[
            pl.BlockSpec(v.shape, lambda n, v=v: (0,) * v.ndim, pipeline_mode=pl.Buffered(1))
            for v in once
        ]
        + [column_spec(v, tile) for v in tiled],
        out_specs=(
            kept_spec,
            kept_spec,
            *halves_spec((shards, extra, tile), width // tile // 2),
            pl.BlockSpec((1, 3 * HS), lambda n: (0, 0)),
        ),
        out_shape=(
            kept,
            kept,
            jax.ShapeDtypeStruct((shards, extra, width // 2), BF16),
            jax.ShapeDtypeStruct((shards, extra, width // 2), BF16),
            jax.ShapeDtypeStruct((1, 3 * HS), F32),
        ),
        scratch_shapes=[
            pltpu.VMEM((length, 3 * HS), BF16),
            pltpu.VMEM((3 * HS, length), BF16),
            pltpu.VMEM((HS, length), BF16),
            pltpu.VMEM((length, HS), F32),
            pltpu.VMEM((length, HS), F32),
        ],
        compiler_params=params_of(56),
        cost_estimate=taking(300),
        name="attend_back",
    )(*once, *tiled)


def halves_spec(block, tiles):
    lead = (0,) * (len(block) - 1)
    return (
        pl.BlockSpec(block, lambda n: lead + (jnp.minimum(n, tiles - 1),)),
        pl.BlockSpec(block, lambda n: lead + (jnp.maximum(n - tiles, 0),)),
    )


def into_halves(refs, store):
    now, tiles = pl.program_id(0), pl.num_programs(0) // 2
    for k, ref in enumerate(refs):
        pl.when(lax.div(now, tiles) == k)(functools.partial(store, ref))


def branch_kernel(c_ref, a_ref, ow_ref, dw_ref, out_ref):
    out_ref[...] = (nn(c_ref[...], ow_ref[...]) + nn(a_ref[...], dw_ref[...])).astype(BF16)


def branch_of(context, active, out_weight, down_weight):
    length, width, tile = context.shape[0], out_weight.shape[1], 256
    return pl.pallas_call(
        branch_kernel,
        grid=(width // tile,),
        in_specs=[
            whole_spec(context),
            whole_spec(active),
            column_spec(out_weight, tile),
            column_spec(down_weight, tile),
        ],
        out_specs=pl.BlockSpec((length, tile), lambda n: (0, n)),
        out_shape=jax.ShapeDtypeStruct((length, width), BF16),
        compiler_params=params_of(32),
        cost_estimate=taking(10),
        name="branch",
    )(context, active, out_weight, down_weight)


def feed_back_kernel(
    g_ref, w_ref, slope_ref, act_ref, two_ref, grads_ref, up_ref, bias_ref, act_t, up_t
):
    now = pl.program_id(0)
    owners, _, rows, tile = grads_ref.shape
    step = w_ref.shape[0]
    steps = act_t.shape[0] // step

    @pl.when(now < steps)
    def _():
        here = pl.ds(pl.multiple_of(now * step, step), step)
        act_t[here] = act_ref[...].T
        up_grad = (nt(g_ref[...], w_ref[...]) * slope_ref[...].astype(F32)).astype(BF16)
        up_ref[...] = up_grad
        bias_ref[...] = jnp.sum(up_grad.astype(F32), axis=0, keepdims=True)
        up_t[here] = up_grad.T

    @pl.when(now >= steps)
    def _():
        g_tile = g_ref[:, pl.ds(pl.multiple_of((now - steps) * tile, tile), tile)]
        grad_down = nn(act_t[...], g_tile).astype(BF16)
        grad_up = nn(up_t[...], two_ref[...]).astype(BF16)
        for k in range(owners):
            grads_ref[k, 0] = grad_down[k * rows : (k + 1) * rows]
            grads_ref[k, 1] = grad_up[k * rows : (k + 1) * rows]


def feed_back(g_all, rows_two, active, slope, down_weight):
    length, width = g_all.shape
    hidden, tile, owners = active.shape[1], 256, 8
    rows = hidden // owners
    step = min(256, hidden)
    steps = hidden // step
    early = lambda n: jnp.minimum(n, steps - 1)
    late = lambda n: jnp.maximum(n - steps, 0)
    units = pl.BlockSpec((length, step), lambda n: (0, early(n)))
    return pl.pallas_call(
        feed_back_kernel,
        grid=(steps + width // tile,),
        in_specs=[
            pl.BlockSpec(g_all.shape, lambda n: (0, 0), pipeline_mode=pl.Buffered(1)),
            pl.BlockSpec((step, width), lambda n: (early(n), 0)),
            units,
            units,
            pl.BlockSpec((length, tile), lambda n: (0, late(n))),
        ],
        out_specs=(
            pl.BlockSpec((owners, 2, rows, tile), lambda n: (0, 0, 0, late(n))),
            units,
            pl.BlockSpec((1, step), lambda n: (0, early(n))),
        ),
        out_shape=(
            jax.ShapeDtypeStruct((owners, 2, rows, width), BF16),
            jax.ShapeDtypeStruct((length, hidden), BF16),
            jax.ShapeDtypeStruct((1, hidden), F32),
        ),
        scratch_shapes=[pltpu.VMEM((hidden, length), BF16), pltpu.VMEM((hidden, length), BF16)],
        compiler_params=params_of(48),
        cost_estimate=taking(80),
        name="feed_back",
    )(g_all, down_weight, slope, active, rows_two)


def sum_spread_kernel(a_ref, b_ref, *out_refs):
    rows = out_refs[0].shape[0]
    me = lax.axis_index("x")
    for by, out_ref in enumerate(out_refs):
        here = pl.ds(pl.multiple_of(lax.rem(me + by, 4) * rows, rows), rows)
        out_ref[...] = (a_ref[here].astype(F32) + b_ref[here].astype(F32)).astype(BF16)


def sum_spread(a, b):
    shape = jax.ShapeDtypeStruct((a.shape[0] // 4, a.shape[1]), BF16)
    return pl.pallas_call(
        sum_spread_kernel,
        out_shape=(shape,) * 4,
        compiler_params=params_of(32),
        cost_estimate=taking(2),
        name="sum_spread",
    )(a, b)


def near_out_kernel(a_ref, in_ref, out_ref):
    step = pl.program_id(0)
    total = a_ref[...].astype(F32)
    blocks = 6

    @pl.when(step < blocks)
    def _():
        in_ref[...] = total

    @pl.when(step >= blocks)
    def _():
        out_ref[...] = total


def near_out(gathered):
    rows, width = gathered.shape[0] // 16, gathered.shape[1]

    def source(n):
        owner = lax.rem(n, 4) * 2 + lax.div(n, 4)
        return (2 * owner + 1, 0)

    return pl.pallas_call(
        near_out_kernel,
        grid=(8,),
        in_specs=[pl.BlockSpec((rows, width), source)],
        out_specs=(
            pl.BlockSpec((rows, width), lambda n: (jnp.minimum(n, 5), 0)),
            pl.BlockSpec((rows, width), lambda n: (jnp.maximum(n - 6, 0), 0)),
        ),
        out_shape=(
            jax.ShapeDtypeStruct((6 * rows, width), F32),
            jax.ShapeDtypeStruct((2 * rows, width), F32),
        ),
        compiler_params=params_of(32),
        cost_estimate=taking(5),
        name="near_out",
    )(gathered)


def widen_kernel(a_ref, out_ref):
    out_ref[...] = a_ref[...].astype(F32)


def widen(v, rows, every):
    width, count = v.shape[1], v.shape[0] // (rows * every)
    return pl.pallas_call(
        widen_kernel,
        grid=(count,),
        in_specs=[pl.BlockSpec((rows, width), lambda n: (every * n, 0))],
        out_specs=pl.BlockSpec((rows, width), lambda n: (n, 0)),
        out_shape=jax.ShapeDtypeStruct((count * rows, width), F32),
        compiler_params=params_of(32),
        cost_estimate=taking(4),
        name="widen",
    )(v)


def swap_sum(v, axis):
    me = lax.axis_index(axis)
    return block(v, me).astype(F32) + shifted(block(v, 1 - me), axis, 1).astype(F32)


def body(
    hidden_in,
    segment_ids,
    positions,
    in_weight,
    out_weight,
    up_weight,
    down_weight,
    in_bias,
    out_bias,
    up_bias,
    down_bias,
    first_gain,
    first_shift,
    second_gain,
    second_shift,
    cotangent,
):
    _, rows, width = hidden_in.shape
    shards = lax.axis_size(SHARD)
    length = rows * shards
    own = width // shards
    me = lax.axis_index(SHARD)
    x_own, g_own = hidden_in[0], cotangent[0]

    owned = own_params(
        [first_gain, first_shift, second_gain, second_shift, out_bias, down_bias], shards
    )
    whole = exchange_blocks(owned)

    whole, x_near, x_far = exchanged(x_own, whole)

    whole = whole.reshape(shards, 6, own).swapaxes(0, 1).reshape(6, width)
    gain_one, shift_one, gain_two, shift_two = (whole[i][None] for i in range(4))
    biases_out = (whole[4] + whole[5])[None]

    seg_col, seg_row = segment_ids[0][:, None], segment_ids
    cosine, sine = angles(positions[0])
    half = jnp.zeros_like(sine)
    rest = jnp.zeros((length, 128 - ROT), F32)
    tables = jnp.stack(
        [
            jnp.concatenate([cosine, cosine, rest + 1.0], axis=-1),
            jnp.concatenate([-sine, half, rest], axis=-1),
            jnp.concatenate([half, sine, rest], axis=-1),
        ]
    )

    buffers = norm_into(x_near, near_places(rows), whole, (), length)
    rows_one, rows_two = norm_into(x_far, far_places(rows), whole, buffers, length)
    g_both, g_left, g_right = exchanged_near(g_own, x_near[3], x_far[2], x_far[3])

    query, keys, values, context, lse = attend(
        rows_one, in_weight, in_bias.astype(F32)[None], seg_col, seg_row, tables
    )

    rows_two, g_left, g_right, context = tie(rows_two, g_left, g_right, context)
    far_top, far_low = exchanged_far(g_left, g_right)
    up = nt(rows_two, up_weight) + up_bias.astype(F32)[None]
    phi = 0.5 * (1.0 + lax.erf(up * (1.0 / math.sqrt(2.0))))
    slope = phi + up * (jnp.exp(-0.5 * up * up) * (1.0 / math.sqrt(2.0 * math.pi)))
    slope = slope.astype(BF16)
    active = (up * phi).astype(BF16)

    active, far_top, far_low = tie(active, far_top, far_low)
    g_all = placed_tokens(g_both, g_left, g_right, far_top, far_low)

    grads, up_grad, up_own = feed_back(g_all, rows_two, active, slope, down_weight)
    part = lax.psum_scatter(grads.reshape(-1, width), CHIP, scatter_dimension=0, tiled=True)

    active, up_grad = tie(active, up_grad)
    branch = branch_of(context, active, out_weight, down_weight)
    context, branch = tie(context, branch)
    branch = exchange_blocks(branch.reshape(shards, rows, width))

    g_late, context, up_grad = tie(g_all, context, up_grad)
    keep, send, inner_one, inner_two, in_own = attend_back(
        g_late, out_weight, query, keys, values, lse, seg_col, seg_row, tables, context, up_grad,
        rows_one, rows_two, in_weight, up_weight, whole,
    )
    heads, hidden = in_own.shape[1], up_own.shape[1]

    near_parts = sum_spread(keep, shifted(send, "c", 1))
    near_pieces = [near_parts[0]] + [shifted(near_parts[by], "x", by) for by in (1, 3, 2)]

    owned_rows = part.shape[0] // 2
    part_down, part_up = part[:owned_rows], part[owned_rows:]
    far_down = shifted(part_down, "zh", 1)
    part_down, part_up, far_down, branch, inner_one, *near_pieces = tie(
        part_down, part_up, far_down, branch, inner_one, *near_pieces
    )
    part_down = add_low(part_down, far_down)
    sum_down = lax.all_gather(part_down, CHIP, axis=0, tiled=True)
    inner_one = exchange_rows(inner_one)
    far_up = shifted(part_up, "zh", 1)
    near = sum(p.astype(F32) for p in near_pieces).astype(BF16)
    near = add_low(near, shifted(near, "zh", 1))
    near, part_up, far_up, inner_one, inner_two, part_down = tie(
        near, part_up, far_up, inner_one, inner_two, part_down
    )
    part_up = add_low(part_up, far_up)
    inner_two = exchange_rows(inner_two)
    late = lax.all_gather(jnp.concatenate([part_up, near]), CHIP, axis=0, tiled=True)
    branch = jnp.sum(branch.astype(F32), axis=0)
    hidden_out = (x_own.astype(F32) + branch + biases_out).astype(BF16)
    inner_one = jnp.sum(inner_one.astype(F32), axis=0).astype(BF16)
    sum_down = widen(sum_down, 256, 1)
    hidden_out, inner_one, inner_two, part_up, sum_down = tie(
        hidden_out, inner_one, inner_two, part_up, sum_down
    )

    inner_two = jnp.sum(inner_two.astype(F32), axis=0).astype(BF16)
    received = jnp.concatenate([inner_one, inner_two], axis=-1).reshape(2, -1, width)
    pair = 2 * lax.axis_index("y") * own
    vectors = lax.dynamic_slice(received[0], (rows, pair), (4, 2 * own)).astype(F32)
    inner_grad = swap_sum(received[:, :rows], "zl")
    vectors = swap_sum(vectors.reshape(4, 2, own).swapaxes(0, 1), "zl")
    xhat_own, scale_own = normed(x_own.astype(F32))
    centered = inner_grad - jnp.mean(inner_grad, axis=-1, keepdims=True)
    along = jnp.mean(inner_grad * xhat_own, axis=-1, keepdims=True)
    grad_hidden = (g_own.astype(F32) + scale_own * (centered - xhat_own * along)).astype(BF16)

    vectors = jnp.stack(
        [
            (vectors[0] - first_shift.astype(F32) * vectors[1]) / first_gain.astype(F32),
            vectors[1],
            (vectors[2] - second_shift.astype(F32) * vectors[3]) / second_gain.astype(F32),
            vectors[3],
        ]
    )
    g_columns = lax.dynamic_slice(g_all, (0, me * own), (length, own))
    small = jnp.concatenate(
        [
            vectors.reshape(-1),
            in_own[0],
            up_own[0],
            jnp.sum(g_columns, axis=0, dtype=F32),
        ]
    )
    small = summed_small(small.reshape(-1, 128), ("c",))
    small, late = tie(small, late)

    small_far = shifted(small, "zh", 1)
    sum_up = widen(late, owned_rows, 2)
    small, small_far, sum_up, grad_hidden, late = tie(small, small_far, sum_up, grad_hidden, late)
    small = small + small_far
    small_far = lax.ppermute(small, "x", [(i, i ^ 2) for i in range(4)])
    sum_in, sum_out = near_out(late)
    small, small_far, sum_in, sum_out = tie(small, small_far, sum_in, sum_out)
    small = small + small_far
    small = small + lax.ppermute(small, "x", [(i, i ^ 1) for i in range(4)])
    small = small.reshape(-1)
    cuts = np.cumsum([own, own, own, own, heads, hidden])
    gain_one_g, shift_one_g, gain_two_g, shift_two_g, in_b, up_b, out_b = jnp.split(small, cuts)

    return (
        hidden_out[None],
        grad_hidden[None],
        sum_in,
        sum_out,
        sum_up,
        sum_down,
        in_b,
        out_b,
        up_b,
        out_b,
        gain_one_g,
        shift_one_g,
        gain_two_g,
        shift_two_g,
    )


def solution(mesh):
    split = Mesh(mesh.devices.reshape(SIZES), AXES)
    tokens, params, vector = P(REPLICA, SHARD, None), P(SHARD, None), P(SHARD)
    return jax.shard_map(
        body,
        mesh=split,
        in_specs=(
            (tokens, P(REPLICA, None), P(REPLICA, None)) + (params,) * 4 + (vector,) * 8 + (tokens,)
        ),
        out_specs=(tokens,) * 2 + (params,) * 4 + (vector,) * 8,
        check_vma=False,
    )
```

```python
import functools
import math

import jax
import jax.numpy as jnp
import numpy as np
from jax import lax
from jax.experimental import pallas as pl
from jax.experimental.pallas import tpu as pltpu
from jax.sharding import Mesh
from jax.sharding import PartitionSpec as P

HS = 256
ROT = 64
EPS = 1e-05
MASKED = -1e30

AXES = ("zh", "x", "c", "y", "zl")
SIZES = (2, 4, 2, 4, 2)
REPLICA = ("zh", "x", "c")
SHARD = ("y", "zl")
CHIP = ("x", "c")

F32 = jnp.float32
BF16 = jnp.bfloat16


def taking(microseconds):
    return pl.CostEstimate(
        flops=int(microseconds * 1e9), bytes_accessed=2**20, transcendentals=0
    )


def params_of(mib):
    return pltpu.CompilerParams(vmem_limit_bytes=mib * 2**20)


def whole_spec(v):
    return pl.BlockSpec(v.shape, lambda *_: (0,) * v.ndim)


def column_spec(v, tile):
    return pl.BlockSpec((v.shape[0], tile), lambda n: (0, n))


def row_spec(v, tile):
    return pl.BlockSpec((tile, v.shape[1]), lambda n: (n, 0))


def shifted(v, axis, by):
    n = lax.axis_size(axis)
    return lax.ppermute(v, axis, [(i, (i + by) % n) for i in range(n)])


def summed_small(v, axes):
    for axis in axes:
        n = lax.axis_size(axis)
        step = n // 2
        while step:
            v = v + lax.ppermute(v, axis, [(i, i ^ step) for i in range(n)])
            step //= 2
    return v


def nt(left, right):
    return lax.dot_general(left, right, (((1,), (1,)), ((), ())), preferred_element_type=F32)


def nn(left, right):
    return lax.dot_general(left, right, (((1,), (0,)), ((), ())), preferred_element_type=F32)


def tn(left, right):
    return lax.dot_general(left, right, (((0,), (0,)), ((), ())), preferred_element_type=F32)


def normed(values):
    center = jnp.mean(values, axis=-1, keepdims=True)
    centered = values - center
    spread = jnp.mean(centered * centered, axis=-1, keepdims=True)
    scale = lax.rsqrt(spread + EPS)
    return centered * scale, scale


def angles(places):
    freq = jnp.power(10000.0, -2.0 * jnp.arange(ROT // 2, dtype=F32) / ROT)
    theta = places.astype(F32)[:, None] * freq
    return jnp.cos(theta), jnp.sin(theta)


def block(v, index):
    return lax.dynamic_index_in_dim(v, index, 0, keepdims=False)


def after(v, *others):
    return lax.optimization_barrier((v,) + others)[0]


def exchanged(own, whole):
    rows = own.shape[0]
    half = rows // 2
    other = shifted(own, "zl", 1)
    left = shifted(own, "y", 1)
    right = shifted(own, "y", -1)
    from_left = shifted(jnp.concatenate([other, left[:half]]), "y", 1)
    from_right = shifted(jnp.concatenate([other, right[half:]]), "y", -1)
    from_left, from_right, whole = tie(from_left, from_right, whole)
    far_top = shifted(from_left[:half], "y", 1)
    far_low = shifted(from_right[half:rows], "y", -1)
    return whole, (own, left, right, other), (from_left, from_right, far_top, far_low)


def near_places(rows):
    return [
        (n, 0, rows, lambda dz=dz, dy=dy: place_of(dz, dy) * rows)
        for n, (dz, dy) in enumerate(((0, 0), (0, 3), (0, 1), (1, 0)))
    ]


def far_places(rows):
    half = rows // 2
    parts = (
        (0, 0, rows, 1, 3, 0),
        (1, 0, rows, 1, 1, 0),
        (0, rows, half, 0, 2, 0),
        (1, rows, half, 0, 2, half),
        (2, 0, half, 1, 2, 0),
        (3, 0, half, 1, 2, half),
    )
    return [
        (n, first, count, lambda dz=dz, dy=dy, low=low: place_of(dz, dy) * rows + low)
        for n, first, count, dz, dy, low in parts
    ]


def exchanged_near(own, ready_z, *ready_y):
    other = shifted(after(own, ready_z), "zl", 1)
    both = after(jnp.stack([own, other]), *ready_y)
    return both, shifted(both, "y", 1), shifted(both, "y", -1)


def exchanged_far(left, right):
    half = left.shape[1] // 2
    return shifted(left[:, :half], "y", 1), shifted(right[:, half:], "y", -1)


def place_kernel(parts, *refs):
    sources, out_ref = refs[:-1], refs[-1]
    for which, inner, place in parts:
        source = sources[which]
        values = source[...] if inner is None else source[inner]
        rows = values.shape[0]
        out_ref[pl.ds(pl.multiple_of(place(), rows), rows)] = values


def placed(sources, parts, rows):
    width, tile = sources[0].shape[-1], 512
    spec = lambda v: pl.BlockSpec(v.shape[:-1] + (tile,), lambda n: (0,) * (v.ndim - 1) + (n,))
    return pl.pallas_call(
        functools.partial(place_kernel, parts),
        grid=(width // tile,),
        in_specs=[spec(v) for v in sources],
        out_specs=pl.BlockSpec((rows, tile), lambda n: (0, n)),
        out_shape=jax.ShapeDtypeStruct((rows, width), sources[0].dtype),
        compiler_params=params_of(57),
        cost_estimate=taking(3),
        name="placed",
    )(*sources)


def placed_tokens(both, left, right, far_top, far_low):
    rows = both.shape[1]
    half = rows // 2
    parts = []
    for dz in range(2):
        for which, dy, low in ((0, 0, 0), (1, 3, 0), (2, 1, 0), (3, 2, 0), (4, 2, half)):
            parts.append(
                (which, dz, lambda dz=dz, dy=dy, low=low: place_of(dz, dy) * rows + low)
            )
    return placed((both, left, right, far_top, far_low), parts, 8 * rows)


def tie(*arrays):
    return lax.optimization_barrier(arrays)


def place_of(dz, dy):
    y, z = lax.axis_index("y"), lax.axis_index("zl")
    return lax.rem(y + dy, 4) * 2 + lax.rem(z + dz, 2)


def own_params_kernel(*refs):
    out_ref = refs[-1]
    for k, ref in enumerate(refs[:-1]):
        size = ref.shape[0]
        row = ref[...].astype(F32).reshape(1, size)
        out_ref[:, k * size : (k + 1) * size] = jnp.broadcast_to(row, (out_ref.shape[0], size))


def own_params(vectors, copies):
    total = sum(v.shape[0] for v in vectors)
    return pl.pallas_call(
        own_params_kernel,
        out_shape=jax.ShapeDtypeStruct((copies, total), F32),
        compiler_params=params_of(32),
        cost_estimate=taking(1),
        name="own_params",
    )(*vectors)


def norm_kernel(pieces, used, *refs):
    x_refs, p_ref = refs[:used], refs[used]
    one_ref, two_ref, one_buf, two_buf, sems = refs[-5:]
    copies = []
    row = 0
    for n, (which, first, rows, place) in enumerate(pieces):
        v = x_refs[which][first : first + rows].astype(F32)
        centered = v - jnp.mean(v, axis=-1, keepdims=True)
        spread = jnp.mean(centered * centered, axis=-1, keepdims=True)
        xhat = centered * lax.rsqrt(spread + EPS)
        here = pl.ds(row, rows)
        one_buf[here] = (xhat * p_ref[0:1] + p_ref[1:2]).astype(BF16)
        two_buf[here] = (xhat * p_ref[2:3] + p_ref[3:4]).astype(BF16)
        there = pl.ds(pl.multiple_of(place(), rows), rows)
        for k, (buf, ref) in enumerate(((one_buf, one_ref), (two_buf, two_ref))):
            copies.append(pltpu.make_async_copy(buf.at[here], ref.at[there], sems.at[2 * n + k]))
            copies[-1].start()
        row += rows
    for copy in copies:
        copy.wait()


def norm_into(arrays, pieces, params, buffers, length):
    width = arrays[0].shape[1]
    total = sum(rows for _, _, rows, _ in pieces)
    any_space = pl.BlockSpec(memory_space=pl.ANY)
    shape = jax.ShapeDtypeStruct((length, width), BF16)
    used = len(arrays)
    return pl.pallas_call(
        functools.partial(norm_kernel, pieces, used),
        in_specs=[pl.BlockSpec(memory_space=pltpu.VMEM)] * (used + 1) + [any_space] * len(buffers),
        out_specs=(any_space, any_space),
        out_shape=(shape, shape),
        input_output_aliases={used + 1: 0, used + 2: 1} if buffers else {},
        scratch_shapes=[
            pltpu.VMEM((total, width), BF16),
            pltpu.VMEM((total, width), BF16),
            pltpu.SemaphoreType.DMA((2 * len(pieces),)),
        ],
        compiler_params=params_of(48),
        cost_estimate=taking(3.4),
        name="norms",
    )(*arrays, params, *buffers)


def add_low(a, b):
    return (a.astype(F32) + b.astype(F32)).astype(BF16)


def exchange_rows(v):
    return lax.all_to_all(v.reshape(4, -1, v.shape[-1]), "y", 0, 0, tiled=True)


def exchange_blocks(v):
    return lax.all_to_all(v, SHARD, 0, 0, tiled=True)


def turn(values, tables, back):
    front = values[:, :128]
    up, down = pltpu.roll(front, 128 - ROT // 2, 1), pltpu.roll(front, ROT // 2, 1)
    moved = up * tables[1] + down * tables[2]
    front = front * tables[0] + (-moved if back else moved)
    return jnp.concatenate([front, values[:, 128:]], axis=-1)


def allowed_of(seg_col, seg_row, start, rows, count):
    same = seg_col[start : start + rows] == seg_row[:, :count]
    query = lax.broadcasted_iota(jnp.int32, (rows, count), 0) + start
    key = lax.broadcasted_iota(jnp.int32, (rows, count), 1)
    return same & (key <= query)


def attend_kernel(x_ref, w_ref, bias_ref, col_ref, row_ref, rot_ref, q_ref, k_ref, v_ref, c_ref, lse_ref):
    step, length = x_ref.shape[0], k_ref.shape[0]
    part = min(256, step)
    mixed = nt(x_ref[...], w_ref[...]) + bias_ref[...]
    tables = [rot_ref[i] for i in range(3)]
    q_ref[...] = (turn(mixed[:, :HS], tables, False) * (1.0 / math.sqrt(HS))).astype(BF16)
    now = pl.program_id(0)
    here = pl.ds(pl.multiple_of(now * step, step), step)
    k_ref[here] = turn(mixed[:, HS : 2 * HS], tables, False).astype(BF16)
    v_ref[here] = mixed[:, 2 * HS :].astype(BF16)
    for first in range(0, length, step):

        @pl.when(now * step == first)
        def _(first=first):
            for inner in range(0, step, part):
                rows, start = pl.ds(inner, part), first + inner
                count = start + part
                scores = nt(q_ref[rows], k_ref[:count])
                allowed = allowed_of(col_ref, row_ref[...], start, part, count)
                scores = jnp.where(allowed, scores, MASKED)
                top = jnp.max(scores, axis=-1, keepdims=True)
                expd = jnp.exp(scores - top)
                total = jnp.sum(expd, axis=-1, keepdims=True)
                probs = (expd * (1.0 / total)).astype(BF16)
                c_ref[rows] = nn(probs, v_ref[:count]).astype(BF16)
                lse_ref[rows] = top + jnp.log(total)


def attend(rows_one, in_weight, bias, seg_col, seg_row, tables):
    length = rows_one.shape[0]
    step = min(512, length)
    head = jax.ShapeDtypeStruct((length, HS), BF16)
    part = pl.BlockSpec((step, HS), lambda n: (n, 0))
    return pl.pallas_call(
        attend_kernel,
        grid=(length // step,),
        in_specs=[
            row_spec(rows_one, step),
            whole_spec(in_weight),
            whole_spec(bias),
            whole_spec(seg_col),
            whole_spec(seg_row),
            pl.BlockSpec((3, step, 128), lambda n: (0, n, 0)),
        ],
        out_specs=(
            part,
            whole_spec(head),
            whole_spec(head),
            part,
            pl.BlockSpec((step, 1), lambda n: (n, 0)),
        ),
        out_shape=(head, head, head, head, jax.ShapeDtypeStruct((length, 1), F32)),
        compiler_params=params_of(48),
        cost_estimate=taking(10),
        name="attend",
    )(rows_one, in_weight, bias, seg_col, seg_row, tables)


def attention_back(
    g_ref, w_ref, q_ref, k_ref, v_ref, lse_ref, col_ref, row_ref, rot_ref, out_ref, dk_ref, dv_ref
):
    length = g_ref.shape[0]
    step = min(256, length)
    seg_row = row_ref[...]
    dk_ref[...] = jnp.zeros_like(dk_ref)
    dv_ref[...] = jnp.zeros_like(dv_ref)
    for start in range(0, length, step):
        here, count = pl.ds(start, step), start + step
        before = pl.ds(0, count)
        context_grad = nt(g_ref[here], w_ref[...]).astype(BF16)
        query = q_ref[here]
        scores = nt(query, k_ref[:count])
        probs = jnp.exp(scores - lse_ref[here])
        probs = jnp.where(allowed_of(col_ref, seg_row, start, step, count), probs, 0.0)
        probs_grad = nt(context_grad, v_ref[:count])
        inner = jnp.sum(probs_grad * probs, axis=-1, keepdims=True)
        score_grad = (probs * (probs_grad - inner)).astype(BF16)
        dv_ref[before] += tn(probs.astype(BF16), context_grad)
        dk_ref[before] += tn(score_grad, query)
        tables = [rot_ref[i, here] for i in range(3)]
        query_grad = turn(nn(score_grad, k_ref[:count]), tables, True)
        out_ref[here, :HS] = (query_grad * (1.0 / math.sqrt(HS))).astype(BF16)
    tables = [rot_ref[i] for i in range(3)]
    out_ref[:, HS : 2 * HS] = turn(dk_ref[...], tables, True).astype(BF16)
    out_ref[:, 2 * HS :] = dv_ref[...].astype(BF16)


def attend_back_kernel(
    g_ref, ow_ref, q_ref, k_ref, v_ref, lse_ref, col_ref, row_ref, rot_ref, c_ref, up_ref,
    one_ref, two_ref, inw_ref, upw_ref, p_ref,
    keep_ref, send_ref, inner_a_ref, inner_b_ref, bias_ref,
    mix_ref, mix_t, c_t, dk_ref, dv_ref,
):
    now = pl.program_id(0)

    @pl.when(now == 0)
    def _():
        attention_back(
            g_ref, ow_ref, q_ref, k_ref, v_ref, lse_ref, col_ref, row_ref, rot_ref, mix_ref, dk_ref, dv_ref
        )
        bias_ref[...] = jnp.sum(mix_ref[...].astype(F32), axis=0, keepdims=True)
        mix_t[...] = mix_ref[...].T
        c_t[...] = c_ref[...].T

    half, tile = keep_ref.shape
    g_tile = g_ref[:, pl.ds(pl.multiple_of(now * tile, tile), tile)]
    one = one_ref[...]
    head = nn(mix_t[:half], one).astype(BF16)
    tail = jnp.concatenate(
        [nn(mix_t[half:], one).astype(BF16), nn(c_t[...], g_tile).astype(BF16)], axis=0
    )
    core = lax.axis_index("c") == 0
    keep_ref[...] = jnp.where(core, head, tail)
    send_ref[...] = jnp.where(core, tail, head)

    blocks, rows = inner_a_ref.shape[0], mix_ref.shape[0] // inner_a_ref.shape[0]
    first = nn(mix_ref[...], inw_ref[...])
    second = nn(up_ref[...], upw_ref[...])
    total = (first * p_ref[0:1] + second * p_ref[2:3]).astype(BF16)
    vectors = [
        jnp.sum(first * one.astype(F32), axis=0, keepdims=True),
        jnp.sum(first, axis=0, keepdims=True),
        jnp.sum(second * two_ref[...].astype(F32), axis=0, keepdims=True),
        jnp.sum(second, axis=0, keepdims=True),
    ]
    extra = jnp.concatenate(vectors + [jnp.zeros((12, tile), F32)], axis=0).astype(BF16)

    def store(ref):
        for k in range(blocks):
            ref[k, :rows] = total[k * rows : (k + 1) * rows]
            ref[k, rows:] = extra

    into_halves((inner_a_ref, inner_b_ref), store)


def attend_back(
    g_all, out_weight, query, keys, values, lse, seg_col, seg_row, tables, context, up_grad,
    rows_one, rows_two, in_weight, up_weight, params,
):
    length, width = rows_one.shape
    shards, tile = 8, 256
    half = (3 * HS + HS) // 2
    extra = length // shards + 16
    kept = jax.ShapeDtypeStruct((half, width), BF16)
    kept_spec = pl.BlockSpec((half, tile), lambda n: (0, n))
    once = [g_all, out_weight, query, keys, values, lse, seg_col, seg_row, tables, context, up_grad]
    tiled = [rows_one, rows_two, in_weight, up_weight, params]
    return pl.pallas_call(
        attend_back_kernel,
        grid=(width // tile,),
        in_specs=[
            pl.BlockSpec(v.shape, lambda n, v=v: (0,) * v.ndim, pipeline_mode=pl.Buffered(1))
            for v in once
        ]
        + [column_spec(v, tile) for v in tiled],
        out_specs=(
            kept_spec,
            kept_spec,
            *halves_spec((shards, extra, tile), width // tile // 2),
            pl.BlockSpec((1, 3 * HS), lambda n: (0, 0)),
        ),
        out_shape=(
            kept,
            kept,
            jax.ShapeDtypeStruct((shards, extra, width // 2), BF16),
            jax.ShapeDtypeStruct((shards, extra, width // 2), BF16),
            jax.ShapeDtypeStruct((1, 3 * HS), F32),
        ),
        scratch_shapes=[
            pltpu.VMEM((length, 3 * HS), BF16),
            pltpu.VMEM((3 * HS, length), BF16),
            pltpu.VMEM((HS, length), BF16),
            pltpu.VMEM((length, HS), F32),
            pltpu.VMEM((length, HS), F32),
        ],
        compiler_params=params_of(56),
        cost_estimate=taking(300),
        name="attend_back",
    )(*once, *tiled)


def halves_spec(block, tiles):
    lead = (0,) * (len(block) - 1)
    return (
        pl.BlockSpec(block, lambda n: lead + (jnp.minimum(n, tiles - 1),)),
        pl.BlockSpec(block, lambda n: lead + (jnp.maximum(n - tiles, 0),)),
    )


def into_halves(refs, store):
    now, tiles = pl.program_id(0), pl.num_programs(0) // 2
    for k, ref in enumerate(refs):
        pl.when(lax.div(now, tiles) == k)(functools.partial(store, ref))


def branch_kernel(c_ref, a_ref, ow_ref, dw_ref, out_ref):
    out_ref[...] = (nn(c_ref[...], ow_ref[...]) + nn(a_ref[...], dw_ref[...])).astype(BF16)


def branch_of(context, active, out_weight, down_weight):
    length, width, tile = context.shape[0], out_weight.shape[1], 512
    return pl.pallas_call(
        branch_kernel,
        grid=(width // tile,),
        in_specs=[
            whole_spec(context),
            whole_spec(active),
            column_spec(out_weight, tile),
            column_spec(down_weight, tile),
        ],
        out_specs=pl.BlockSpec((length, tile), lambda n: (0, n)),
        out_shape=jax.ShapeDtypeStruct((length, width), BF16),
        compiler_params=params_of(57),
        cost_estimate=taking(10),
        name="branch",
    )(context, active, out_weight, down_weight)


def feed_back_kernel(
    g_ref, w_ref, slope_ref, act_ref, two_ref, grads_ref, up_ref, bias_ref, act_t, up_t
):
    now = pl.program_id(0)
    owners, _, rows, tile = grads_ref.shape
    step = w_ref.shape[0]
    steps = act_t.shape[0] // step

    @pl.when(now < steps)
    def _():
        here = pl.ds(pl.multiple_of(now * step, step), step)
        act_t[here] = act_ref[...].T
        up_grad = (nt(g_ref[...], w_ref[...]) * slope_ref[...].astype(F32)).astype(BF16)
        up_ref[...] = up_grad
        bias_ref[...] = jnp.sum(up_grad.astype(F32), axis=0, keepdims=True)
        up_t[here] = up_grad.T

    @pl.when(now >= steps)
    def _():
        g_tile = g_ref[:, pl.ds(pl.multiple_of((now - steps) * tile, tile), tile)]
        grad_down = nn(act_t[...], g_tile).astype(BF16)
        grad_up = nn(up_t[...], two_ref[...]).astype(BF16)
        for k in range(owners):
            grads_ref[k, 0] = grad_down[k * rows : (k + 1) * rows]
            grads_ref[k, 1] = grad_up[k * rows : (k + 1) * rows]


def feed_back(g_all, rows_two, active, slope, down_weight):
    length, width = g_all.shape
    hidden, tile, owners = active.shape[1], 256, 8
    rows = hidden // owners
    step = min(256, hidden)
    steps = hidden // step
    early = lambda n: jnp.minimum(n, steps - 1)
    late = lambda n: jnp.maximum(n - steps, 0)
    units = pl.BlockSpec((length, step), lambda n: (0, early(n)))
    return pl.pallas_call(
        feed_back_kernel,
        grid=(steps + width // tile,),
        in_specs=[
            pl.BlockSpec(g_all.shape, lambda n: (0, 0), pipeline_mode=pl.Buffered(1)),
            pl.BlockSpec((step, width), lambda n: (early(n), 0)),
            units,
            units,
            pl.BlockSpec((length, tile), lambda n: (0, late(n))),
        ],
        out_specs=(
            pl.BlockSpec((owners, 2, rows, tile), lambda n: (0, 0, 0, late(n))),
            units,
            pl.BlockSpec((1, step), lambda n: (0, early(n))),
        ),
        out_shape=(
            jax.ShapeDtypeStruct((owners, 2, rows, width), BF16),
            jax.ShapeDtypeStruct((length, hidden), BF16),
            jax.ShapeDtypeStruct((1, hidden), F32),
        ),
        scratch_shapes=[pltpu.VMEM((hidden, length), BF16), pltpu.VMEM((hidden, length), BF16)],
        compiler_params=params_of(57),
        cost_estimate=taking(80),
        name="feed_back",
    )(g_all, down_weight, slope, active, rows_two)


def sum_spread_kernel(a_ref, b_ref, *out_refs):
    rows = out_refs[0].shape[0]
    me = lax.axis_index("x")
    for by, out_ref in enumerate(out_refs):
        here = pl.ds(pl.multiple_of(lax.rem(me + by, 4) * rows, rows), rows)
        out_ref[...] = (a_ref[here].astype(F32) + b_ref[here].astype(F32)).astype(BF16)


def sum_spread(a, b):
    shape = jax.ShapeDtypeStruct((a.shape[0] // 4, a.shape[1]), BF16)
    return pl.pallas_call(
        sum_spread_kernel,
        out_shape=(shape,) * 4,
        compiler_params=params_of(32),
        cost_estimate=taking(2),
        name="sum_spread",
    )(a, b)


def near_out_kernel(a_ref, in_ref, out_ref):
    step = pl.program_id(0)
    total = a_ref[...].astype(F32)
    blocks = 6

    @pl.when(step < blocks)
    def _():
        in_ref[...] = total

    @pl.when(step >= blocks)
    def _():
        out_ref[...] = total


def near_out(gathered):
    rows, width = gathered.shape[0] // 16, gathered.shape[1]

    def source(n):
        owner = lax.rem(n, 4) * 2 + lax.div(n, 4)
        return (2 * owner + 1, 0)

    return pl.pallas_call(
        near_out_kernel,
        grid=(8,),
        in_specs=[pl.BlockSpec((rows, width), source)],
        out_specs=(
            pl.BlockSpec((rows, width), lambda n: (jnp.minimum(n, 5), 0)),
            pl.BlockSpec((rows, width), lambda n: (jnp.maximum(n - 6, 0), 0)),
        ),
        out_shape=(
            jax.ShapeDtypeStruct((6 * rows, width), F32),
            jax.ShapeDtypeStruct((2 * rows, width), F32),
        ),
        compiler_params=params_of(32),
        cost_estimate=taking(5),
        name="near_out",
    )(gathered)


def widen_kernel(a_ref, out_ref):
    out_ref[...] = a_ref[...].astype(F32)


def widen(v, rows, every):
    width, count = v.shape[1], v.shape[0] // (rows * every)
    return pl.pallas_call(
        widen_kernel,
        grid=(count,),
        in_specs=[pl.BlockSpec((rows, width), lambda n: (every * n, 0))],
        out_specs=pl.BlockSpec((rows, width), lambda n: (n, 0)),
        out_shape=jax.ShapeDtypeStruct((count * rows, width), F32),
        compiler_params=params_of(57),
        cost_estimate=taking(4),
        name="widen",
    )(v)


def swap_sum(v, axis):
    me = lax.axis_index(axis)
    return block(v, me).astype(F32) + shifted(block(v, 1 - me), axis, 1).astype(F32)


def body(
    hidden_in,
    segment_ids,
    positions,
    in_weight,
    out_weight,
    up_weight,
    down_weight,
    in_bias,
    out_bias,
    up_bias,
    down_bias,
    first_gain,
    first_shift,
    second_gain,
    second_shift,
    cotangent,
):
    _, rows, width = hidden_in.shape
    shards = lax.axis_size(SHARD)
    length = rows * shards
    own = width // shards
    me = lax.axis_index(SHARD)
    x_own, g_own = hidden_in[0], cotangent[0]

    owned = own_params(
        [first_gain, first_shift, second_gain, second_shift, out_bias, down_bias], shards
    )
    whole = exchange_blocks(owned)

    whole, x_near, x_far = exchanged(x_own, whole)

    whole = whole.reshape(shards, 6, own).swapaxes(0, 1).reshape(6, width)
    gain_one, shift_one, gain_two, shift_two = (whole[i][None] for i in range(4))
    biases_out = (whole[4] + whole[5])[None]

    seg_col, seg_row = segment_ids[0][:, None], segment_ids
    cosine, sine = angles(positions[0])
    half = jnp.zeros_like(sine)
    rest = jnp.zeros((length, 128 - ROT), F32)
    tables = jnp.stack(
        [
            jnp.concatenate([cosine, cosine, rest + 1.0], axis=-1),
            jnp.concatenate([-sine, half, rest], axis=-1),
            jnp.concatenate([half, sine, rest], axis=-1),
        ]
    )

    buffers = norm_into(x_near, near_places(rows), whole, (), length)
    rows_one, rows_two = norm_into(x_far, far_places(rows), whole, buffers, length)
    g_both, g_left, g_right = exchanged_near(g_own, x_near[3], x_far[2], x_far[3])

    query, keys, values, context, lse = attend(
        rows_one, in_weight, in_bias.astype(F32)[None], seg_col, seg_row, tables
    )

    rows_two, g_left, g_right, context = tie(rows_two, g_left, g_right, context)
    far_top, far_low = exchanged_far(g_left, g_right)
    up = nt(rows_two, up_weight) + up_bias.astype(F32)[None]
    phi = 0.5 * (1.0 + lax.erf(up * (1.0 / math.sqrt(2.0))))
    slope = phi + up * (jnp.exp(-0.5 * up * up) * (1.0 / math.sqrt(2.0 * math.pi)))
    slope = slope.astype(BF16)
    active = (up * phi).astype(BF16)

    active, far_top, far_low = tie(active, far_top, far_low)
    g_all = placed_tokens(g_both, g_left, g_right, far_top, far_low)

    grads, up_grad, up_own = feed_back(g_all, rows_two, active, slope, down_weight)
    part = lax.psum_scatter(grads.reshape(-1, width), CHIP, scatter_dimension=0, tiled=True)

    active, up_grad = tie(active, up_grad)
    branch = branch_of(context, active, out_weight, down_weight)
    context, branch = tie(context, branch)
    branch = exchange_blocks(branch.reshape(shards, rows, width))

    g_late, context, up_grad = tie(g_all, context, up_grad)
    keep, send, inner_one, inner_two, in_own = attend_back(
        g_late, out_weight, query, keys, values, lse, seg_col, seg_row, tables, context, up_grad,
        rows_one, rows_two, in_weight, up_weight, whole,
    )
    heads, hidden = in_own.shape[1], up_own.shape[1]

    near_parts = sum_spread(keep, shifted(send, "c", 1))
    near_pieces = [near_parts[0]] + [shifted(near_parts[by], "x", by) for by in (1, 3, 2)]

    owned_rows = part.shape[0] // 2
    part_down, part_up = part[:owned_rows], part[owned_rows:]
    far_down = shifted(part_down, "zh", 1)
    part_down, part_up, far_down, branch, inner_one, *near_pieces = tie(
        part_down, part_up, far_down, branch, inner_one, *near_pieces
    )
    part_down = add_low(part_down, far_down)
    sum_down = lax.all_gather(part_down, CHIP, axis=0, tiled=True)
    inner_one = exchange_rows(inner_one)
    far_up = shifted(part_up, "zh", 1)
    near = sum(p.astype(F32) for p in near_pieces).astype(BF16)
    near = add_low(near, shifted(near, "zh", 1))
    near, part_up, far_up, inner_one, inner_two, part_down = tie(
        near, part_up, far_up, inner_one, inner_two, part_down
    )
    part_up = add_low(part_up, far_up)
    inner_two = exchange_rows(inner_two)
    late = lax.all_gather(jnp.concatenate([part_up, near]), CHIP, axis=0, tiled=True)
    branch = jnp.sum(branch.astype(F32), axis=0)
    hidden_out = (x_own.astype(F32) + branch + biases_out).astype(BF16)
    inner_one = jnp.sum(inner_one.astype(F32), axis=0).astype(BF16)
    sum_down = widen(sum_down, 256, 1)
    hidden_out, inner_one, inner_two, part_up, sum_down = tie(
        hidden_out, inner_one, inner_two, part_up, sum_down
    )

    inner_two = jnp.sum(inner_two.astype(F32), axis=0).astype(BF16)
    received = jnp.concatenate([inner_one, inner_two], axis=-1).reshape(2, -1, width)
    pair = 2 * lax.axis_index("y") * own
    vectors = lax.dynamic_slice(received[0], (rows, pair), (4, 2 * own)).astype(F32)
    inner_grad = swap_sum(received[:, :rows], "zl")
    vectors = swap_sum(vectors.reshape(4, 2, own).swapaxes(0, 1), "zl")
    xhat_own, scale_own = normed(x_own.astype(F32))
    centered = inner_grad - jnp.mean(inner_grad, axis=-1, keepdims=True)
    along = jnp.mean(inner_grad * xhat_own, axis=-1, keepdims=True)
    grad_hidden = (g_own.astype(F32) + scale_own * (centered - xhat_own * along)).astype(BF16)

    vectors = jnp.stack(
        [
            (vectors[0] - first_shift.astype(F32) * vectors[1]) / first_gain.astype(F32),
            vectors[1],
            (vectors[2] - second_shift.astype(F32) * vectors[3]) / second_gain.astype(F32),
            vectors[3],
        ]
    )
    g_columns = lax.dynamic_slice(g_all, (0, me * own), (length, own))
    small = jnp.concatenate(
        [
            vectors.reshape(-1),
            in_own[0],
            up_own[0],
            jnp.sum(g_columns, axis=0, dtype=F32),
        ]
    )
    small = summed_small(small.reshape(-1, 128), ("c",))
    small, late = tie(small, late)

    small_far = shifted(small, "zh", 1)
    sum_up = widen(late, owned_rows, 2)
    small, small_far, sum_up, grad_hidden, late = tie(small, small_far, sum_up, grad_hidden, late)
    small = small + small_far
    small_far = lax.ppermute(small, "x", [(i, i ^ 2) for i in range(4)])
    sum_in, sum_out = near_out(late)
    small, small_far, sum_in, sum_out = tie(small, small_far, sum_in, sum_out)
    small = small + small_far
    small = small + lax.ppermute(small, "x", [(i, i ^ 1) for i in range(4)])
    small = small.reshape(-1)
    cuts = np.cumsum([own, own, own, own, heads, hidden])
    gain_one_g, shift_one_g, gain_two_g, shift_two_g, in_b, up_b, out_b = jnp.split(small, cuts)

    return (
        hidden_out[None],
        grad_hidden[None],
        sum_in,
        sum_out,
        sum_up,
        sum_down,
        in_b,
        out_b,
        up_b,
        out_b,
        gain_one_g,
        shift_one_g,
        gain_two_g,
        shift_two_g,
    )


def solution(mesh):
    split = Mesh(mesh.devices.reshape(SIZES), AXES)
    tokens, params, vector = P(REPLICA, SHARD, None), P(SHARD, None), P(SHARD)
    return jax.shard_map(
        body,
        mesh=split,
        in_specs=(
            (tokens, P(REPLICA, None), P(REPLICA, None)) + (params,) * 4 + (vector,) * 8 + (tokens,)
        ),
        out_specs=(tokens,) * 2 + (params,) * 4 + (vector,) * 8,
        check_vma=False,
    )
```
